512 devices in a mesh: row: 16 (over y, x_hi), col: 32 (over z, x_lo, core).
Axes of the slice: x: 4 (x_hi: 2, x_lo: 2; x = x_hi * 2 + x_lo), y: 8, z: 8, core: 2. Of those that a mesh axis runs over, the one named last changes fastest.
Arguments:
- pair: bfloat16 [768, 768, 128], P('row', 'col'), may hold values from -6 to 6
- token_mask: int32 [768], replicated, may hold values 0 or 1
- ln_gain: float32 [128], replicated, may hold values from 0.25 to 1.75
- ln_bias: float32 [128], replicated, may hold values from -3 to 3
- w_left: bfloat16 [128, 128], replicated, may hold values from -0.5 to 0.5
- w_right: bfloat16 [128, 128], replicated, may hold values from -0.5 to 0.5
- w_gate: bfloat16 [128, 128], replicated, may hold values from -0.5 to 0.5
- w_out: bfloat16 [64, 128], replicated, may hold values from -1.5 to 1.5
Outputs:
- update: bfloat16 [768, 768, 128], P('row', 'col')
The draws below stay inside these ranges and needn't reach their ends.
All inputs are finite; a program needn't handle non-finite values.
Results may differ from the reference program's by a relative error of at most 0.0053.
Values may be sent and summed in bfloat16 or wider, within the bound.
A program may use at most 64 MiB of HBM per device.

```python
import math
import jax
import jax.numpy as jnp
from jax import lax

D = 128
CH = 64
TOKENS = 768


def plant(entries, own_key, low, largest):
    dims = entries.shape
    place = [jax.random.randint(jax.random.fold_in(own_key, axis), (), 0, dims[axis]) for axis in range(len(dims))]
    entries = entries.at[tuple(place)].set(low)
    longest = dims.index(max(dims))
    place[longest] = (place[longest] + 1) % dims[longest]
    return entries.at[tuple(place)].set(largest)


def block_levels(rng, extent, split, low, top_value):
    level = 1.0
    for dim, parts in split:
        steps = jax.random.uniform(jax.random.fold_in(jax.random.fold_in(rng, 6), dim), (parts,), jnp.float32, low / len(split), top_value / len(split))
        level = level * jnp.repeat(jnp.exp(steps), extent[dim] // parts).reshape((-1,) + (1,) * (len(extent) - 1 - dim))
    return level


def scatter_about(key, dims, scale, reach, split=(), kind=jnp.bfloat16):
    drawn = jax.random.normal(key, dims, jnp.float32) * scale
    if len(split) > 0:
        drawn = block_levels(key, dims, split, -0.22, 0.18) * drawn
    return jnp.clip(drawn, min=-reach, max=reach).astype(kind)


def setup_inputs(seed: int = 0) -> dict:
    keys = jax.random.split(jax.random.key(seed), 9)
    return {
        "pair": scatter_about(keys[0], (TOKENS, TOKENS, D), 1.0, 6.0, ((0, 16), (1, 32))),
        "token_mask": plant((jax.random.randint(keys[1], (TOKENS,), 0, 8) < 7).astype(jnp.int32), jax.random.fold_in(keys[1], 1), 0, 1),
        "ln_gain": jnp.clip(1.0 + 0.15 * jax.random.normal(keys[2], (D,), jnp.float32), 0.25, 1.75),
        "ln_bias": scatter_about(keys[3], (D,), 0.5, 3.0, (), jnp.float32),
        "w_left": scatter_about(keys[4], (D, 2 * CH), D ** -0.5, 0.5),
        "w_right": scatter_about(keys[5], (D, 2 * CH), D ** -0.5, 0.5),
        "w_gate": scatter_about(keys[6], (D, D), D ** -0.5, 0.5),
        "w_out": scatter_about(keys[7], (CH, D), (CH // 4) ** -0.5, 1.5),
    }


def normalize(block, ln_gain, ln_bias):
    values = block.astype(jnp.float32)
    center = lax.optimization_barrier(jnp.mean(values, axis=-1, keepdims=True))
    spread = lax.optimization_barrier(jnp.mean((values - center) ** 2, axis=-1, keepdims=True))
    return ((values - center) / jnp.sqrt(spread + 1e-05) * ln_gain + ln_bias).astype(jnp.bfloat16)

def activate(normed, weight, masks):
    rows, cols, width = normed.shape
    proj = jnp.dot(normed.reshape(rows * cols, width), weight, preferred_element_type=jnp.float32)
    proj = proj.reshape(rows, cols, 2 * CH)
    return (jax.nn.sigmoid(proj[:, :, :CH]) * proj[:, :, CH:] * masks[:, :, None]).astype(jnp.bfloat16)

def reference(pair, token_mask, ln_gain, ln_bias, w_left, w_right, w_gate, w_out):
    block = math.gcd(TOKENS, 128)
    count = TOKENS // block
    maskf = token_mask.astype(jnp.float32)

    def first(index):
        start = index * block
        rows = lax.dynamic_slice_in_dim(pair, start, block, 0)
        normed = normalize(rows, ln_gain, ln_bias)
        masks = lax.dynamic_slice_in_dim(maskf, start, block, 0)[:, None] * maskf[None, :]
        return (activate(normed, w_left, masks), activate(normed, w_right, masks))
    left_all, right_all = lax.map(first, jnp.arange(count, dtype=jnp.int32))
    left_all = left_all.reshape(TOKENS, TOKENS, CH)
    right_all = right_all.reshape(TOKENS, TOKENS, CH).astype(jnp.float32)
    scale = 4.0 / math.sqrt(TOKENS)

    def second(index):
        start = index * block
        rows = lax.dynamic_slice_in_dim(pair, start, block, 0)
        normed = normalize(rows, ln_gain, ln_bias)
        left_rows = lax.dynamic_slice_in_dim(left_all, start, block, 0).astype(jnp.float32)
        tri = (scale * jnp.einsum('ikc,jkc->ijc', left_rows, right_all)).astype(jnp.bfloat16)
        flat = normed.reshape(block * TOKENS, D)
        gate = jax.nn.sigmoid(jnp.dot(flat, w_gate, preferred_element_type=jnp.float32))
        mixed = jnp.dot(tri.reshape(block * TOKENS, CH), w_out, preferred_element_type=jnp.float32)
        return (gate * mixed).astype(jnp.bfloat16).reshape(block, TOKENS, D)
    update = lax.map(second, jnp.arange(count, dtype=jnp.int32))
    return update.reshape(TOKENS, TOKENS, D)
```

```python
import functools
import math

import jax
import jax.numpy as jnp
from jax import lax
from jax.experimental import pallas as pl
from jax.experimental.pallas import tpu as pltpu
from jax.sharding import PartitionSpec as P

F32 = jnp.float32
BF16 = jnp.bfloat16
MESH = pl.DeviceIdType.MESH


def one_hot(shape, source):
    row = lax.broadcasted_iota(jnp.int32, shape, 0)
    col = lax.broadcasted_iota(jnp.int32, shape, 1)
    return row, col, source(row)


def permutation(count, source):
    _, col, src = one_hot((count, count), source)
    return jnp.where(col == src, 1.0, 0.0).astype(BF16)


def swap_ends(a, b, c):
    return permutation(a * b * c, lambda o: (o % a) * (b * c) + ((o // a) % b) * c + o // (a * b))


def nt_dot(x, y):
    return lax.dot_general(x, y, (((1,), (1,)), ((), ())), preferred_element_type=F32)


def tn_dot(x, y):
    return lax.dot_general(x, y, (((0,), (0,)), ((), ())), preferred_element_type=F32)


def nn_dot(x, y):
    return lax.dot_general(x, y, (((1,), (0,)), ((), ())), preferred_element_type=F32)


def exchange(parts, width):
    n = len(parts)
    total = n * width
    pos = lax.broadcasted_iota(jnp.int32, parts[0].shape, 1) // width
    rolled = [parts[0]] + [pltpu.roll(parts[y], y * width, 1) for y in range(1, n)]
    result = []
    for k in range(n):
        picked = rolled[0]
        for y in range(1, n):
            picked = jnp.where(pos == (k + y) % n, rolled[y], picked)
        result.append(picked if k == 0 else pltpu.roll(picked, total - k * width, 1))
    return result


def fold(block):
    third = block.shape[1] // 3
    a, b, c = (block[:, i * third:(i + 1) * third] for i in range(3))
    return jnp.concatenate(
        [jnp.concatenate([a, b], 0), jnp.concatenate([c, jnp.zeros_like(c)], 0)], 1
    )


def unfold(block):
    n, third = block.shape[0] // 2, block.shape[1] // 2
    return jnp.concatenate([block[:n, :third], block[n:, :third], block[:n, third:]], 1)


def kernel(
    ny, nz, tm, pair, gain, bias, w_left, w_right, w_gate, w_out, out,
    n32, normed, gate, wt, a1, b1, a2, b2, lx, rs, rx, pp, qq, sa, fa, ga, ha, sb, fb, gb, hb,
    s1, r1, s2, r2, sl, rl, sr, rr, sq, rq, s3, r3, s4, r4,
):
    rows, cols, width = pair.shape
    nt = cols // ny
    lanes = ny * rows
    chans = ny * nz
    row, col = lax.axis_index("row"), lax.axis_index("col")
    y, xh = row // 2, row % 2
    z, xl, core = col // 4, (col // 2) % 2, col % 2
    same = xl == xh

    def at_y(d):
        return lax.rem(y + d, ny)

    def at_z(d):
        return lax.rem(z + d, nz)

    def dev_y(other):
        return (other * 2 + xh, col)

    def dev_z(other):
        return (row, other * 4 + xl * 2 + core)

    def dev_x(oh, ol):
        return (y * 2 + oh, z * 4 + ol * 2 + core)

    other_core = (row, z * 4 + xl * 2 + 1 - core)
    peers = [dev_y(at_y(d)) for d in range(1, ny)] + [dev_z(at_z(d)) for d in range(1, nz)]
    peers += [dev_x(xh, 1 - xl), dev_x(1 - xh, xl), dev_x(1 - xh, 1 - xl), other_core]
    barrier = pltpu.get_barrier_semaphore()
    for peer in peers:
        pl.semaphore_signal(barrier, inc=1, device_id=peer, device_id_type=MESH)

    def send(src, dst, send_sem, recv_sem, device):
        pltpu.make_async_remote_copy(
            src_ref=src, dst_ref=dst, send_sem=send_sem, recv_sem=recv_sem,
            device_id=device, device_id_type=MESH,
        ).start()

    def take(ref, sem):
        pltpu.make_async_copy(ref, ref, sem).wait()

    def weight_rows(offset):
        total = None
        for side, weight in ((0, w_left), (1, w_right)):
            r, c, src = one_hot(
                (2 * chans, 2 * chans), lambda o: (o // (2 * nz)) * nz + o % nz + offset
            )
            pick = jnp.where((c == src) & ((r // nz) % 2 == side), 1.0, 0.0).astype(BF16)
            part = nt_dot(pick, weight[...])
            total = part if total is None else total + part
        return total.astype(BF16)

    wt[0:2 * chans, :] = weight_rows(0)
    wt[2 * chans:4 * chans, :] = weight_rows(chans)

    lane = lax.broadcasted_iota(jnp.int32, (1, lanes), 1)
    row_mask = jnp.zeros((1, lanes), F32)
    for i in range(rows):
        row_mask = jnp.where(lane % rows == i, tm[row * rows + i].astype(F32), row_mask)

    def mask_of(t):
        col_mask = jnp.zeros((1, lanes), F32)
        for k in range(ny):
            col_mask = jnp.where(lane // rows == k, tm[col * cols + t * ny + k].astype(F32), col_mask)
        return row_mask * col_mask

    def project(t):
        block = pair[:, t * ny:(t + 1) * ny, :].astype(F32)
        center = jnp.mean(block, axis=-1, keepdims=True)
        delta = block - center
        spread = jnp.mean(delta * delta, axis=-1, keepdims=True)
        value = delta * lax.rsqrt(spread + 1e-05) * gain[...].reshape(1, 1, width) + bias[...].reshape(1, 1, width)
        n32[t] = value.reshape(rows * ny, width)
        for k in range(ny):
            normed[t, k * rows:(k + 1) * rows, :] = n32[t, pl.ds(k, rows, stride=ny), :].astype(BF16)
        proj = nt_dot(wt[...], normed[t])
        act = jax.nn.sigmoid(proj[:2 * chans]) * proj[2 * chans:] * mask_of(t)
        a1[t] = act.astype(BF16).reshape(ny, 2 * nz, lanes)

    def send_y(t):
        for d in range(1, ny):
            to = at_y(d)
            send(a1.at[t, to], b1.at[t, y], s1.at[t], r1.at[t], dev_y(to))
        b1[t, y] = a1[t, y]

    swap1 = swap_ends(ny, 2, nz)

    def turn(t):
        take(b1.at[t, pl.ds(0, ny - 1)], r1.at[t])
        parts = exchange([b1[t, k].astype(F32) for k in range(ny)], rows)
        stacked = jnp.concatenate(parts, 0).astype(BF16)
        a2[t] = nn_dot(swap1, stacked).astype(BF16).reshape(nz, 2 * ny, lanes)
        for d in range(1, nz):
            to = at_z(d)
            send(a2.at[t, to], b2.at[t, z], s2.at[t], r2.at[t], dev_z(to))
        b2[t, z] = a2[t, z]

    def spread_x(t):
        take(b2.at[t, pl.ds(0, nz - 1)], r2.at[t])
        both = b2[t].astype(F32).reshape(nz, 2, ny, lanes)
        lx[xl, t] = both[:, 0].reshape(nz * ny, lanes).astype(BF16)
        send(lx.at[xl, t], lx.at[xl, t], sl.at[t], rl.at[t], dev_x(xh, 1 - xl))
        right = both[:, 1].reshape(nz * ny, lanes).astype(BF16)
        rs[t] = right
        send(rs.at[t], rx.at[xl, t], sr.at[t], rr.at[t], dev_x(1 - xh, xh))

        @pl.when(same)
        def _():
            rx[xl, t] = right

        @pl.when(jnp.logical_not(same))
        def _():
            send(rs.at[t], rx.at[xl, t], sr.at[t], rr.at[t], dev_x(xh, xh))

    def gather_x(t):
        take(lx.at[0, t], rl.at[t])

        @pl.when(same)
        def _():
            take(rx.at[0, t], rr.at[t])

        @pl.when(jnp.logical_not(same))
        def _():
            take(rx.at[:, t], rr.at[t])

    project(0)
    pl.semaphore_wait(barrier, len(peers))
    send_y(0)
    for t in range(1, nt):
        project(t)
        send_y(t)
    turn(0)
    turn(1)
    spread_x(0)
    turn(2)
    spread_x(1)
    for t in range(nt):
        gate[t] = jax.nn.sigmoid(nn_dot(normed[t], w_gate[...]))
    spread_x(2)

    half = nz * ny * 2
    gather_x(0)
    gather_x(1)
    first = tn_dot(rx[:, 0:2].reshape(2 * half, lanes), lx[:, 0:2].reshape(2 * half, lanes))
    gather_x(2)
    total = first + tn_dot(rx[:, 2].reshape(half, lanes), lx[:, 2].reshape(half, lanes))
    pp[...] = total.reshape(nz, rows, lanes)
    send(pp.at[:, pl.ds((1 - core) * cols, cols), :], qq, sq, rq, other_core)
    take(qq, rq)
    scale = 4.0 / math.sqrt(rows * 2 * ny)
    two = 2 * ny

    tri = (pp[:, pl.ds(core * cols, cols), :] + qq[...]) * scale
    sa[...] = tri[:, :two].astype(BF16)
    for d in range(1, nz):
        to = at_z(d)
        send(sa.at[to], fa.at[z], s3.at[0], r3.at[0], dev_z(to))
    for k in range(nz):
        sb[k] = fold(tri[k, two:]).astype(BF16)
    for d in range(1, nz):
        to = at_z(d)
        send(sb.at[to], fb.at[z], s3.at[1], r3.at[1], dev_z(to))
    fa[z] = sa[z]
    fb[z] = sb[z]

    take(fa.at[pl.ds(0, nz - 1)], r3.at[0])
    turned = nn_dot(swap_ends(nz, 2, ny), fa[...].reshape(nz * two, lanes)).reshape(ny, 2 * nz, lanes)
    parts = exchange([turned[j] for j in range(ny)], rows)
    for k in range(ny):
        ga[k] = parts[k].astype(BF16)
    for d in range(1, ny):
        to = at_y(d)
        send(ga.at[to], ha.at[y], s4.at[0], r4.at[0], dev_y(to))
    ha[y] = ga[y]

    take(fb.at[pl.ds(0, nz - 1)], r3.at[1])
    flat = jnp.concatenate([unfold(fb[k].astype(F32)) for k in range(nz)], 0).astype(BF16)
    turned = nn_dot(swap_ends(nz, 1, ny), flat).reshape(ny, nz, lanes)
    parts = exchange([turned[j] for j in range(ny)], rows)
    for k in range(ny):
        gb[k] = fold(parts[k]).astype(BF16)
    for d in range(1, ny):
        to = at_y(d)
        send(gb.at[to], hb.at[y], s4.at[1], r4.at[1], dev_y(to))
    hb[y] = gb[y]

    def finish(t, block):
        mixed = tn_dot(block.reshape(chans, lanes).astype(BF16), w_out[...])
        out[t * ny:(t + 1) * ny] = (gate[t] * mixed).astype(BF16).reshape(ny, rows, width)

    take(ha.at[pl.ds(0, ny - 1)], r4.at[0])
    both = ha[...].astype(F32).reshape(ny, 2, nz, lanes)
    finish(0, both[:, 0])
    finish(1, both[:, 1])
    take(hb.at[pl.ds(0, ny - 1)], r4.at[1])
    finish(2, jnp.concatenate([unfold(hb[k].astype(F32)) for k in range(ny)], 0))

    for t in range(nt):
        take(a1.at[t, pl.ds(0, ny - 1)], s1.at[t])
        take(a2.at[t, pl.ds(0, nz - 1)], s2.at[t])
        take(lx.at[0, t], sl.at[t])

        @pl.when(same)
        def _():
            take(rx.at[0, t], sr.at[t])

        @pl.when(jnp.logical_not(same))
        def _():
            take(rx.at[:, t], sr.at[t])
    take(qq, sq)
    take(sa.at[pl.ds(0, nz - 1)], s3.at[0])
    take(sb.at[pl.ds(0, nz - 1)], s3.at[1])
    take(ga.at[pl.ds(0, ny - 1)], s4.at[0])
    take(gb.at[pl.ds(0, ny - 1)], s4.at[1])


def per_device(ny, nz, pair, token_mask, ln_gain, ln_bias, w_left, w_right, w_gate, w_out):
    rows, cols, width = pair.shape
    lanes = ny * rows
    nt = cols // ny
    chans = ny * nz
    third = 2 * lanes // 3
    dma = pltpu.SemaphoreType.DMA
    vmem = pl.BlockSpec(memory_space=pltpu.VMEM)
    swapped = pl.pallas_call(
        functools.partial(kernel, ny, nz),
        out_shape=jax.ShapeDtypeStruct((cols, rows, width), BF16),
        in_specs=[pl.BlockSpec(memory_space=pltpu.SMEM)] + [vmem] * 7,
        out_specs=vmem,
        scratch_shapes=[
            pltpu.VMEM((nt, rows * ny, width), F32),
            pltpu.VMEM((nt, rows * ny, width), BF16),
            pltpu.VMEM((nt, rows * ny, width), F32),
            pltpu.VMEM((4 * chans, width), BF16),
            pltpu.VMEM((nt, ny, 2 * nz, lanes), BF16),
            pltpu.VMEM((nt, ny, 2 * nz, lanes), BF16),
            pltpu.VMEM((nt, nz, 2 * ny, lanes), BF16),
            pltpu.VMEM((nt, nz, 2 * ny, lanes), BF16),
            pltpu.VMEM((2, nt, nz * ny, lanes), BF16),
            pltpu.VMEM((nt, nz * ny, lanes), BF16),
            pltpu.VMEM((2, nt, nz * ny, lanes), BF16),
            pltpu.VMEM((nz, rows, lanes), F32),
            pltpu.VMEM((nz, cols, lanes), F32),
            pltpu.VMEM((nz, 2 * ny, lanes), BF16),
            pltpu.VMEM((nz, 2 * ny, lanes), BF16),
            pltpu.VMEM((ny, 2 * nz, lanes), BF16),
            pltpu.VMEM((ny, 2 * nz, lanes), BF16),
            pltpu.VMEM((nz, 2 * ny, third), BF16),
            pltpu.VMEM((nz, 2 * ny, third), BF16),
            pltpu.VMEM((ny, 2 * nz, third), BF16),
            pltpu.VMEM((ny, 2 * nz, third), BF16),
        ] + [dma((nt,))] * 8 + [dma, dma] + [dma((2,))] * 4,
        compiler_params=pltpu.CompilerParams(
            collective_id=0, has_side_effects=True, vmem_limit_bytes=48 * 1024 * 1024
        ),
    )(token_mask, pair, ln_gain.reshape(1, width), ln_bias.reshape(1, width), w_left, w_right, w_gate, w_out)
    return jnp.transpose(swapped, (1, 0, 2))


def solution(mesh):
    ny, nz = mesh.shape["row"] // 2, mesh.shape["col"] // 4
    placed = (P("row", "col", None), P(), P(), P(), P(), P(), P(), P())
    return jax.shard_map(
        functools.partial(per_device, ny, nz), mesh=mesh, in_specs=placed,
        out_specs=P("row", "col", None), check_vma=False,
    )
```

```python
import functools
import math

import jax
import jax.numpy as jnp
from jax import lax
from jax.experimental import pallas as pl
from jax.experimental.pallas import tpu as pltpu
from jax.sharding import PartitionSpec as P

F32 = jnp.float32
BF16 = jnp.bfloat16
MESH = pl.DeviceIdType.MESH


def one_hot(shape, source):
    row = lax.broadcasted_iota(jnp.int32, shape, 0)
    col = lax.broadcasted_iota(jnp.int32, shape, 1)
    return row, col, source(row)


def permutation(count, source):
    _, col, src = one_hot((count, count), source)
    return jnp.where(col == src, 1.0, 0.0).astype(BF16)


def swap_ends(a, b, c):
    return permutation(a * b * c, lambda o: (o % a) * (b * c) + ((o // a) % b) * c + o // (a * b))


def far_first(n):
    return sorted(range(1, n), key=lambda d: -min(d, n - d))


def nt_dot(x, y):
    return lax.dot_general(x, y, (((1,), (1,)), ((), ())), preferred_element_type=F32)


def tn_dot(x, y):
    return lax.dot_general(x, y, (((0,), (0,)), ((), ())), preferred_element_type=F32)


def nn_dot(x, y):
    return lax.dot_general(x, y, (((1,), (0,)), ((), ())), preferred_element_type=F32)


def exchange(parts, width):
    n = len(parts)
    total = n * width
    pos = lax.broadcasted_iota(jnp.int32, parts[0].shape, 1) // width
    rolled = [parts[0]] + [pltpu.roll(parts[y], y * width, 1) for y in range(1, n)]
    result = []
    for k in range(n):
        picked = rolled[0]
        for y in range(1, n):
            picked = jnp.where(pos == (k + y) % n, rolled[y], picked)
        result.append(picked if k == 0 else pltpu.roll(picked, total - k * width, 1))
    return result


def fold(block):
    third = block.shape[1] // 3
    a, b, c = (block[:, i * third:(i + 1) * third] for i in range(3))
    return jnp.concatenate(
        [jnp.concatenate([a, b], 0), jnp.concatenate([c, jnp.zeros_like(c)], 0)], 1
    )


def unfold(block):
    n, third = block.shape[0] // 2, block.shape[1] // 2
    return jnp.concatenate([block[:n, :third], block[n:, :third], block[:n, third:]], 1)


def kernel(
    ny, nz, tm_hbm, pair_hbm, gain_hbm, bias_hbm, wl_hbm, wr_hbm, wg_hbm, wo_hbm, out,
    tm, pair, gain, bias, w_left, w_right, w_gate, w_out, load, n32, normed, gate, wt, a1, b1, a2, b2, lx, rs, rx, pp, qq, sa, fa, ga, ha, sb, fb, gb, hb,
    s1, r1, s2, r2, sl, rl, sr, rr, sq, rq, s3, r3, s4, r4,
):
    rows, cols, width = pair.shape
    nt = cols // ny
    lanes = ny * rows
    chans = ny * nz
    loads = [
        pltpu.make_async_copy(src, dst, load.at[i])
        for i, (src, dst) in enumerate((
            (pair_hbm, pair), (wl_hbm, w_left), (wr_hbm, w_right), (tm_hbm, tm),
            (gain_hbm, gain), (bias_hbm, bias), (wg_hbm, w_gate), (wo_hbm, w_out),
        ))
    ]
    row, col = lax.axis_index("row"), lax.axis_index("col")
    y, xh = row // 2, row % 2
    z, xl, core = col // 4, (col // 2) % 2, col % 2
    same = xl == xh

    def at_y(d):
        return lax.rem(y + d, ny)

    def at_z(d):
        return lax.rem(z + d, nz)

    def dev_y(other):
        return (other * 2 + xh, col)

    def dev_z(other):
        return (row, other * 4 + xl * 2 + core)

    def dev_x(oh, ol):
        return (y * 2 + oh, z * 4 + ol * 2 + core)

    other_core = (row, z * 4 + xl * 2 + 1 - core)
    peers = [dev_y(at_y(d)) for d in range(1, ny)] + [dev_z(at_z(d)) for d in range(1, nz)]
    peers += [dev_x(xh, 1 - xl), dev_x(1 - xh, xl), dev_x(1 - xh, 1 - xl), other_core]
    barrier = pltpu.get_barrier_semaphore()
    for peer in peers:
        pl.semaphore_signal(barrier, inc=1, device_id=peer, device_id_type=MESH)

    for copy in loads:
        copy.start()

    def send(src, dst, send_sem, recv_sem, device):
        pltpu.make_async_remote_copy(
            src_ref=src, dst_ref=dst, send_sem=send_sem, recv_sem=recv_sem,
            device_id=device, device_id_type=MESH,
        ).start()

    def take(ref, sem):
        pltpu.make_async_copy(ref, ref, sem).wait()

    for copy in loads[1:]:
        copy.wait()

    def weight_rows(offset):
        total = None
        for side, weight in ((0, w_left), (1, w_right)):
            r, c, src = one_hot(
                (2 * chans, 2 * chans), lambda o: (o // (2 * nz)) * nz + o % nz + offset
            )
            pick = jnp.where((c == src) & ((r // nz) % 2 == side), 1.0, 0.0).astype(BF16)
            part = nt_dot(pick, weight[...])
            total = part if total is None else total + part
        return total.astype(BF16)

    wt[0:2 * chans, :] = weight_rows(0)
    wt[2 * chans:4 * chans, :] = weight_rows(chans)

    lane = lax.broadcasted_iota(jnp.int32, (1, lanes), 1)
    row_mask = jnp.zeros((1, lanes), F32)
    for i in range(rows):
        row_mask = jnp.where(lane % rows == i, tm[row * rows + i].astype(F32), row_mask)

    def mask_of(t):
        col_mask = jnp.zeros((1, lanes), F32)
        for k in range(ny):
            col_mask = jnp.where(lane // rows == k, tm[col * cols + t * ny + k].astype(F32), col_mask)
        return row_mask * col_mask

    def project(t):
        block = pair[:, t * ny:(t + 1) * ny, :].astype(F32)
        center = jnp.mean(block, axis=-1, keepdims=True)
        delta = block - center
        spread = jnp.mean(delta * delta, axis=-1, keepdims=True)
        value = delta * lax.rsqrt(spread + 1e-05) * gain[...].reshape(1, 1, width) + bias[...].reshape(1, 1, width)
        n32[t] = value.reshape(rows * ny, width)
        for k in range(ny):
            normed[t, k * rows:(k + 1) * rows, :] = n32[t, pl.ds(k, rows, stride=ny), :].astype(BF16)
        proj = nt_dot(wt[...], normed[t])
        act = jax.nn.sigmoid(proj[:2 * chans]) * proj[2 * chans:] * mask_of(t)
        a1[t] = act.astype(BF16).reshape(ny, 2 * nz, lanes)

    def send_y(t):
        for d in far_first(ny):
            to = at_y(d)
            send(a1.at[t, to], b1.at[t, y], s1.at[t], r1.at[t], dev_y(to))
        b1[t, y] = a1[t, y]

    swap1 = swap_ends(ny, 2, nz)

    def turn(t):
        take(b1.at[t, pl.ds(0, ny - 1)], r1.at[t])
        parts = exchange([b1[t, k].astype(F32) for k in range(ny)], rows)
        stacked = jnp.concatenate(parts, 0).astype(BF16)
        a2[t] = nn_dot(swap1, stacked).astype(BF16).reshape(nz, 2 * ny, lanes)
        for d in far_first(nz):
            to = at_z(d)
            send(a2.at[t, to], b2.at[t, z], s2.at[t], r2.at[t], dev_z(to))
        b2[t, z] = a2[t, z]

    def spread_x(t):
        take(b2.at[t, pl.ds(0, nz - 1)], r2.at[t])
        both = b2[t].astype(F32).reshape(nz, 2, ny, lanes)
        lx[xl, t] = both[:, 0].reshape(nz * ny, lanes).astype(BF16)
        send(lx.at[xl, t], lx.at[xl, t], sl.at[t], rl.at[t], dev_x(xh, 1 - xl))
        right = both[:, 1].reshape(nz * ny, lanes).astype(BF16)
        rs[t] = right
        send(rs.at[t], rx.at[xl, t], sr.at[t], rr.at[t], dev_x(1 - xh, xh))

        @pl.when(same)
        def _():
            rx[xl, t] = right

        @pl.when(jnp.logical_not(same))
        def _():
            send(rs.at[t], rx.at[xl, t], sr.at[t], rr.at[t], dev_x(xh, xh))

    def gather_x(t):
        take(lx.at[0, t], rl.at[t])

        @pl.when(same)
        def _():
            take(rx.at[0, t], rr.at[t])

        @pl.when(jnp.logical_not(same))
        def _():
            take(rx.at[:, t], rr.at[t])

    loads[0].wait()
    project(0)
    pl.semaphore_wait(barrier, len(peers))
    send_y(0)
    for t in range(1, nt):
        project(t)
        send_y(t)
    turn(0)
    turn(1)
    spread_x(0)
    turn(2)
    spread_x(1)
    for t in range(nt):
        gate[t] = jax.nn.sigmoid(nn_dot(normed[t], w_gate[...]))
    spread_x(2)

    half = nz * ny * 2
    gather_x(0)
    gather_x(1)
    first = tn_dot(rx[:, 0:2].reshape(2 * half, lanes), lx[:, 0:2].reshape(2 * half, lanes))
    gather_x(2)
    total = first + tn_dot(rx[:, 2].reshape(half, lanes), lx[:, 2].reshape(half, lanes))
    pp[...] = total.reshape(nz, rows, lanes)
    send(pp.at[:, pl.ds((1 - core) * cols, cols), :], qq, sq, rq, other_core)
    take(qq, rq)
    scale = 4.0 / math.sqrt(rows * 2 * ny)
    two = 2 * ny

    tri = (pp[:, pl.ds(core * cols, cols), :] + qq[...]) * scale
    sa[...] = tri[:, :two].astype(BF16)
    for d in far_first(nz):
        to = at_z(d)
        send(sa.at[to], fa.at[z], s3.at[0], r3.at[0], dev_z(to))
    for k in range(nz):
        sb[k] = fold(tri[k, two:]).astype(BF16)
    for d in far_first(nz):
        to = at_z(d)
        send(sb.at[to], fb.at[z], s3.at[1], r3.at[1], dev_z(to))
    fa[z] = sa[z]
    fb[z] = sb[z]

    take(fa.at[pl.ds(0, nz - 1)], r3.at[0])
    turned = nn_dot(swap_ends(nz, 2, ny), fa[...].reshape(nz * two, lanes)).reshape(ny, 2 * nz, lanes)
    parts = exchange([turned[j] for j in range(ny)], rows)
    for k in range(ny):
        ga[k] = parts[k].astype(BF16)
    for d in far_first(ny):
        to = at_y(d)
        send(ga.at[to], ha.at[y], s4.at[0], r4.at[0], dev_y(to))
    ha[y] = ga[y]

    take(fb.at[pl.ds(0, nz - 1)], r3.at[1])
    flat = jnp.concatenate([unfold(fb[k].astype(F32)) for k in range(nz)], 0).astype(BF16)
    turned = nn_dot(swap_ends(nz, 1, ny), flat).reshape(ny, nz, lanes)
    parts = exchange([turned[j] for j in range(ny)], rows)
    for k in range(ny):
        gb[k] = fold(parts[k]).astype(BF16)
    for d in far_first(ny):
        to = at_y(d)
        send(gb.at[to], hb.at[y], s4.at[1], r4.at[1], dev_y(to))
    hb[y] = gb[y]

    def finish(t, block):
        mixed = tn_dot(block.reshape(chans, lanes).astype(BF16), w_out[...])
        out[t * ny:(t + 1) * ny] = (gate[t] * mixed).astype(BF16).reshape(ny, rows, width)

    take(ha.at[pl.ds(0, ny - 1)], r4.at[0])
    both = ha[...].astype(F32).reshape(ny, 2, nz, lanes)
    finish(0, both[:, 0])
    finish(1, both[:, 1])
    take(hb.at[pl.ds(0, ny - 1)], r4.at[1])
    finish(2, jnp.concatenate([unfold(hb[k].astype(F32)) for k in range(ny)], 0))

    for t in range(nt):
        take(a1.at[t, pl.ds(0, ny - 1)], s1.at[t])
        take(a2.at[t, pl.ds(0, nz - 1)], s2.at[t])
        take(lx.at[0, t], sl.at[t])

        @pl.when(same)
        def _():
            take(rx.at[0, t], sr.at[t])

        @pl.when(jnp.logical_not(same))
        def _():
            take(rx.at[:, t], sr.at[t])
    take(qq, sq)
    take(sa.at[pl.ds(0, nz - 1)], s3.at[0])
    take(sb.at[pl.ds(0, nz - 1)], s3.at[1])
    take(ga.at[pl.ds(0, ny - 1)], s4.at[0])
    take(gb.at[pl.ds(0, ny - 1)], s4.at[1])


def per_device(ny, nz, pair, token_mask, ln_gain, ln_bias, w_left, w_right, w_gate, w_out):
    rows, cols, width = pair.shape
    lanes = ny * rows
    nt = cols // ny
    chans = ny * nz
    third = 2 * lanes // 3
    dma = pltpu.SemaphoreType.DMA
    swapped = pl.pallas_call(
        functools.partial(kernel, ny, nz),
        out_shape=jax.ShapeDtypeStruct((cols, rows, width), BF16),
        in_specs=[pl.BlockSpec(memory_space=pl.ANY)] * 8,
        out_specs=pl.BlockSpec(memory_space=pltpu.VMEM),
        scratch_shapes=[
            pltpu.SMEM(token_mask.shape, jnp.int32),
            pltpu.VMEM(pair.shape, BF16),
            pltpu.VMEM((1, width), F32),
            pltpu.VMEM((1, width), F32),
            pltpu.VMEM(w_left.shape, BF16),
            pltpu.VMEM(w_right.shape, BF16),
            pltpu.VMEM(w_gate.shape, BF16),
            pltpu.VMEM(w_out.shape, BF16),
            dma((8,)),
            pltpu.VMEM((nt, rows * ny, width), F32),
            pltpu.VMEM((nt, rows * ny, width), BF16),
            pltpu.VMEM((nt, rows * ny, width), F32),
            pltpu.VMEM((4 * chans, width), BF16),
            pltpu.VMEM((nt, ny, 2 * nz, lanes), BF16),
            pltpu.VMEM((nt, ny, 2 * nz, lanes), BF16),
            pltpu.VMEM((nt, nz, 2 * ny, lanes), BF16),
            pltpu.VMEM((nt, nz, 2 * ny, lanes), BF16),
            pltpu.VMEM((2, nt, nz * ny, lanes), BF16),
            pltpu.VMEM((nt, nz * ny, lanes), BF16),
            pltpu.VMEM((2, nt, nz * ny, lanes), BF16),
            pltpu.VMEM((nz, rows, lanes), F32),
            pltpu.VMEM((nz, cols, lanes), F32),
            pltpu.VMEM((nz, 2 * ny, lanes), BF16),
            pltpu.VMEM((nz, 2 * ny, lanes), BF16),
            pltpu.VMEM((ny, 2 * nz, lanes), BF16),
            pltpu.VMEM((ny, 2 * nz, lanes), BF16),
            pltpu.VMEM((nz, 2 * ny, third), BF16),
            pltpu.VMEM((nz, 2 * ny, third), BF16),
            pltpu.VMEM((ny, 2 * nz, third), BF16),
            pltpu.VMEM((ny, 2 * nz, third), BF16),
        ] + [dma((nt,))] * 8 + [dma, dma] + [dma((2,))] * 4,
        compiler_params=pltpu.CompilerParams(
            collective_id=0, has_side_effects=True, vmem_limit_bytes=64 * 1024 * 1024
        ),
    )(token_mask, pair, ln_gain.reshape(1, width), ln_bias.reshape(1, width), w_left, w_right, w_gate, w_out)
    return jnp.transpose(swapped, (1, 0, 2))


def solution(mesh):
    ny, nz = mesh.shape["row"] // 2, mesh.shape["col"] // 4
    placed = (P("row", "col", None), P(), P(), P(), P(), P(), P(), P())
    return jax.shard_map(
        functools.partial(per_device, ny, nz), mesh=mesh, in_specs=placed,
        out_specs=P("row", "col", None), check_vma=False,
    )
```

```python
import functools
import math

import jax
import jax.numpy as jnp
from jax import lax
from jax.experimental import pallas as pl
from jax.experimental.pallas import tpu as pltpu
from jax.sharding import PartitionSpec as P

F32 = jnp.float32
BF16 = jnp.bfloat16
MESH = pl.DeviceIdType.MESH


def one_hot(shape, source):
    row = lax.broadcasted_iota(jnp.int32, shape, 0)
    col = lax.broadcasted_iota(jnp.int32, shape, 1)
    return row, col, source(row)


def permutation(count, source):
    _, col, src = one_hot((count, count), source)
    return jnp.where(col == src, 1.0, 0.0).astype(BF16)


def swap_ends(a, b, c):
    return permutation(a * b * c, lambda o: (o % a) * (b * c) + ((o // a) % b) * c + o // (a * b))


def far_first(n):
    return sorted(range(1, n), key=lambda d: -min(d, n - d))


def nt_dot(x, y):
    return lax.dot_general(x, y, (((1,), (1,)), ((), ())), preferred_element_type=F32)


def tn_dot(x, y):
    return lax.dot_general(x, y, (((0,), (0,)), ((), ())), preferred_element_type=F32)


def nn_dot(x, y):
    return lax.dot_general(x, y, (((1,), (0,)), ((), ())), preferred_element_type=F32)


def exchange(parts, width):
    n = len(parts)
    total = n * width
    pos = lax.broadcasted_iota(jnp.int32, parts[0].shape, 1) // width
    rolled = [parts[0]] + [pltpu.roll(parts[y], y * width, 1) for y in range(1, n)]
    result = []
    for k in range(n):
        picked = rolled[0]
        for y in range(1, n):
            picked = jnp.where(pos == (k + y) % n, rolled[y], picked)
        result.append(picked if k == 0 else pltpu.roll(picked, total - k * width, 1))
    return result


def fold(block):
    third = block.shape[1] // 3
    a, b, c = (block[:, i * third:(i + 1) * third] for i in range(3))
    return jnp.concatenate(
        [jnp.concatenate([a, b], 0), jnp.concatenate([c, jnp.zeros_like(c)], 0)], 1
    )


def unfold(block):
    n, third = block.shape[0] // 2, block.shape[1] // 2
    return jnp.concatenate([block[:n, :third], block[n:, :third], block[:n, third:]], 1)


def kernel(
    ny, nz, tm_hbm, pair_hbm, gain_hbm, bias_hbm, wl_hbm, wr_hbm, wg_hbm, wo_hbm, out,
    tm, pair, gain, bias, w_left, w_right, w_gate, w_out, load, n32, normed, gate, wt,
    a1l, a1lf, b1l, b1lf, a1r, a1rf, b1r, b1rf, a2l, a2lf, b2l, b2lf, a2r, a2rf, b2r, b2rf, rx, rxf,
    pp, qq, sa, fa, ga, ha, sb, fb, gb, hb,
    s1l, r1l, s1r, r1r, s2l, r2l, s2r, r2r, sl, rl, sr, rr, sq, rq, s3, r3, s4, r4,
):
    rows, cols, width = pair.shape
    nt = cols // ny
    lanes = ny * rows
    chans = ny * nz
    loads = [
        pltpu.make_async_copy(src, dst, load.at[i])
        for i, (src, dst) in enumerate((
            (pair_hbm, pair), (wl_hbm, w_left), (wr_hbm, w_right), (tm_hbm, tm),
            (gain_hbm, gain), (bias_hbm, bias), (wg_hbm, w_gate), (wo_hbm, w_out),
        ))
    ]
    row, col = lax.axis_index("row"), lax.axis_index("col")
    y, xh = row // 2, row % 2
    z, xl, core = col // 4, (col // 2) % 2, col % 2
    same = xl == xh

    def at_y(d):
        return lax.rem(y + d, ny)

    def at_z(d):
        return lax.rem(z + d, nz)

    def dev_y(other):
        return (other * 2 + xh, col)

    def dev_z(other):
        return (row, other * 4 + xl * 2 + core)

    def dev_x(oh, ol):
        return (y * 2 + oh, z * 4 + ol * 2 + core)

    other_core = (row, z * 4 + xl * 2 + 1 - core)
    peers = [dev_y(at_y(d)) for d in far_first(ny)] + [dev_z(at_z(d)) for d in far_first(nz)]
    peers += [dev_x(xh, 1 - xl), dev_x(1 - xh, xl), dev_x(1 - xh, 1 - xl), other_core]
    barrier = pltpu.get_barrier_semaphore()
    for peer in peers:
        pl.semaphore_signal(barrier, inc=1, device_id=peer, device_id_type=MESH)

    for copy in loads:
        copy.start()

    def send(src, dst, send_sem, recv_sem, device):
        pltpu.make_async_remote_copy(
            src_ref=src, dst_ref=dst, send_sem=send_sem, recv_sem=recv_sem,
            device_id=device, device_id_type=MESH,
        ).start()

    def take(ref, sem):
        pltpu.make_async_copy(ref, ref, sem).wait()

    for copy in loads[1:]:
        copy.wait()

    _, c, r = one_hot((2 * chans, 2 * chans), lambda o: o)
    wt[0:2 * chans, :] = nt_dot(jnp.where(c == r, 1.0, 0.0).astype(BF16), w_left[...]).astype(BF16)
    _, c, r = one_hot(
        (2 * chans, 2 * chans), lambda o: (o // chans) * chans + (o % ny) * nz + (o % chans) // ny
    )
    wt[2 * chans:4 * chans, :] = nt_dot(jnp.where(c == r, 1.0, 0.0).astype(BF16), w_right[...]).astype(BF16)

    lane = lax.broadcasted_iota(jnp.int32, (1, lanes), 1)
    row_mask = jnp.zeros((1, lanes), F32)
    for i in range(rows):
        row_mask = jnp.where(lane % rows == i, tm[row * rows + i].astype(F32), row_mask)

    def mask_of(t):
        col_mask = jnp.zeros((1, lanes), F32)
        for k in range(ny):
            col_mask = jnp.where(lane // rows == k, tm[col * cols + t * ny + k].astype(F32), col_mask)
        return row_mask * col_mask

    def project(t):
        block = pair[:, t * ny:(t + 1) * ny, :].astype(F32)
        center = jnp.mean(block, axis=-1, keepdims=True)
        delta = block - center
        spread = jnp.mean(delta * delta, axis=-1, keepdims=True)
        value = delta * lax.rsqrt(spread + 1e-05) * gain[...].reshape(1, 1, width) + bias[...].reshape(1, 1, width)
        n32[t] = value.reshape(rows * ny, width)
        for k in range(ny):
            normed[t, k * rows:(k + 1) * rows, :] = n32[t, pl.ds(k, rows, stride=ny), :].astype(BF16)
        proj = nt_dot(wt[...], normed[t])
        mask = mask_of(t)
        sides = (proj[:2 * chans], proj[2 * chans:])
        return [jax.nn.sigmoid(side[:chans]) * side[chans:] * mask for side in sides]

    swap1 = swap_ends(ny, 2, nz)
    swap2 = swap_ends(ny, 1, nz)

    def send_first(left, left_land, right, right_land, part):
        for d in far_first(ny):
            to = at_y(d)
            send(left.at[to], left_land.at[y], s1l.at[part], r1l.at[part], dev_y(to))
        for d in far_first(nz):
            to = at_z(d)
            send(right.at[to], right_land.at[z], s1r.at[part], r1r.at[part], dev_z(to))
        left_land[y] = left[y]
        right_land[z] = right[z]

    loads[0].wait()
    left0, right0 = project(0)
    left1, right1 = project(1)
    pairs = lambda u, v, n: jnp.concatenate([u.reshape(n, -1, lanes), v.reshape(n, -1, lanes)], 1).astype(BF16)
    a1l[...] = pairs(left0, left1, ny)
    a1r[...] = pairs(right0, right1, nz)
    pl.semaphore_wait(barrier, len(peers))
    send_first(a1l, b1l, a1r, b1r, 0)
    left2, right2 = project(2)
    for k in range(ny):
        a1lf[k] = fold(left2[k * nz:(k + 1) * nz]).astype(BF16)
    for k in range(nz):
        a1rf[k] = fold(right2[k * ny:(k + 1) * ny]).astype(BF16)
    send_first(a1lf, b1lf, a1rf, b1rf, 1)

    def turn_right(land, part, out_buf, dst):
        take(land.at[pl.ds(0, nz - 1)], r1r.at[part])
        out_buf[...] = nn_dot(swap1, land[...].reshape(nz * 2 * ny, -1)).astype(BF16).reshape(out_buf.shape)
        for d in far_first(ny):
            to = at_y(d)
            send(out_buf.at[to], dst.at[y], s2r.at[part], r2r.at[part, y], dev_y(to))
        dst[y] = out_buf[y]

    def send_left(out_buf, dst, part):
        for d in far_first(nz):
            to = at_z(d)
            send(out_buf.at[to], dst.at[xl, z], s2l.at[part], r2l.at[part, z], dev_z(to))
        dst[xl, z] = out_buf[z]

    turn_right(b1r, 0, a2r, b2r)
    take(b1l.at[pl.ds(0, ny - 1)], r1l.at[0])
    parts = exchange([b1l[k].astype(F32) for k in range(ny)], rows)
    a2l[...] = nn_dot(swap1, jnp.concatenate(parts, 0).astype(BF16)).astype(BF16).reshape(a2l.shape)
    send_left(a2l, b2l, 0)
    turn_right(b1rf, 1, a2rf, b2rf)
    take(b1lf.at[pl.ds(0, ny - 1)], r1l.at[1])
    parts = exchange([unfold(b1lf[k].astype(F32)) for k in range(ny)], rows)
    turned = nn_dot(swap2, jnp.concatenate(parts, 0).astype(BF16))
    for k in range(nz):
        a2lf[k] = fold(turned[k * ny:(k + 1) * ny]).astype(BF16)
    send_left(a2lf, b2lf, 1)

    for t in range(nt):
        gate[t] = jax.nn.sigmoid(nn_dot(normed[t], w_gate[...]))

    def forward(left, right, right_dst, part):
        def forward_left(k):
            send(left.at[xl, k], left.at[xl, k], sl.at[part], rl.at[part], dev_x(xh, 1 - xl))

        def forward_right(k):
            send(right.at[k], right_dst.at[xl, k], sr.at[part], rr.at[part], dev_x(1 - xh, xh))

            @pl.when(jnp.logical_not(same))
            def _():
                send(right.at[k], right_dst.at[xl, k], sr.at[part], rr.at[part], dev_x(xh, xh))

        forward_right(y)
        forward_left(z)
        for d in reversed(far_first(ny)):
            k = at_y(d)
            take(right.at[k], r2r.at[part, k])
            forward_right(k)
            k = at_z(d)
            take(left.at[xl, k], r2l.at[part, k])
            forward_left(k)

        @pl.when(same)
        def _():
            right_dst[xl] = right[...]

    def gather_x(left, right_dst, part):
        take(left.at[0], rl.at[part])

        @pl.when(same)
        def _():
            take(right_dst.at[0], rr.at[part])

        @pl.when(jnp.logical_not(same))
        def _():
            take(right_dst, rr.at[part])

    forward(b2l, b2r, rx, 0)
    forward(b2lf, b2rf, rxf, 1)

    two = 2 * ny
    gather_x(b2l, rx, 0)
    panels = []
    for x in range(2):
        parts = exchange([rx[x, k].astype(F32) for k in range(ny)], rows)
        panels.append(nn_dot(swap1, jnp.concatenate(parts, 0).astype(BF16)).astype(BF16))
    total = tn_dot(jnp.concatenate(panels, 0), b2l[...].reshape(2 * nz * two, lanes))
    gather_x(b2lf, rxf, 1)
    panels = []
    for x in range(2):
        parts = exchange([unfold(rxf[x, k].astype(F32)) for k in range(ny)], rows)
        panels.append(nn_dot(swap2, jnp.concatenate(parts, 0).astype(BF16)).astype(BF16))
    lefts = [unfold(b2lf[x, k].astype(F32)) for x in range(2) for k in range(nz)]
    total = total + tn_dot(jnp.concatenate(panels, 0), jnp.concatenate(lefts, 0).astype(BF16))
    pp[...] = total.reshape(nz, rows, lanes)
    send(pp.at[:, pl.ds((1 - core) * cols, cols), :], qq, sq, rq, other_core)
    take(qq, rq)
    scale = 4.0 / math.sqrt(rows * 2 * ny)

    tri = (pp[:, pl.ds(core * cols, cols), :] + qq[...]) * scale
    sa[...] = tri[:, :two].astype(BF16)
    for d in far_first(nz):
        to = at_z(d)
        send(sa.at[to], fa.at[z], s3.at[0], r3.at[0], dev_z(to))
    for k in range(nz):
        sb[k] = fold(tri[k, two:]).astype(BF16)
    for d in far_first(nz):
        to = at_z(d)
        send(sb.at[to], fb.at[z], s3.at[1], r3.at[1], dev_z(to))
    fa[z] = sa[z]
    fb[z] = sb[z]

    take(fa.at[pl.ds(0, nz - 1)], r3.at[0])
    turned = nn_dot(swap_ends(nz, 2, ny), fa[...].reshape(nz * two, lanes)).reshape(ny, 2 * nz, lanes)
    parts = exchange([turned[j] for j in range(ny)], rows)
    for k in range(ny):
        ga[k] = parts[k].astype(BF16)
    for d in far_first(ny):
        to = at_y(d)
        send(ga.at[to], ha.at[y], s4.at[0], r4.at[0], dev_y(to))
    ha[y] = ga[y]

    take(fb.at[pl.ds(0, nz - 1)], r3.at[1])
    flat = jnp.concatenate([unfold(fb[k].astype(F32)) for k in range(nz)], 0).astype(BF16)
    turned = nn_dot(swap_ends(nz, 1, ny), flat).reshape(ny, nz, lanes)
    parts = exchange([turned[j] for j in range(ny)], rows)
    for k in range(ny):
        gb[k] = fold(parts[k]).astype(BF16)
    for d in far_first(ny):
        to = at_y(d)
        send(gb.at[to], hb.at[y], s4.at[1], r4.at[1], dev_y(to))
    hb[y] = gb[y]

    def finish(t, block):
        mixed = tn_dot(block.reshape(chans, lanes).astype(BF16), w_out[...])
        out[t * ny:(t + 1) * ny] = (gate[t] * mixed).astype(BF16).reshape(ny, rows, width)

    take(ha.at[pl.ds(0, ny - 1)], r4.at[0])
    both = ha[...].astype(F32).reshape(ny, 2, nz, lanes)
    finish(0, both[:, 0])
    finish(1, both[:, 1])
    take(hb.at[pl.ds(0, ny - 1)], r4.at[1])
    finish(2, jnp.concatenate([unfold(hb[k].astype(F32)) for k in range(ny)], 0))

    for part, (first, second, land) in enumerate(((a1l, a2l, rx), (a1lf, a2lf, rxf))):
        take(first.at[pl.ds(0, ny - 1)], s1l.at[part])
        take(first.at[pl.ds(0, nz - 1)], s1r.at[part])
        take(second.at[pl.ds(0, nz - 1)], s2l.at[part])
        take(second.at[pl.ds(0, ny - 1)], s2r.at[part])
        take(land.at[0], sl.at[part])

        @pl.when(same)
        def _():
            take(land.at[0], sr.at[part])

        @pl.when(jnp.logical_not(same))
        def _():
            take(land, sr.at[part])
    take(qq, sq)
    take(sa.at[pl.ds(0, nz - 1)], s3.at[0])
    take(sb.at[pl.ds(0, nz - 1)], s3.at[1])
    take(ga.at[pl.ds(0, ny - 1)], s4.at[0])
    take(gb.at[pl.ds(0, ny - 1)], s4.at[1])


def per_device(ny, nz, pair, token_mask, ln_gain, ln_bias, w_left, w_right, w_gate, w_out):
    rows, cols, width = pair.shape
    lanes = ny * rows
    nt = cols // ny
    chans = ny * nz
    third = 2 * lanes // 3
    dma = pltpu.SemaphoreType.DMA
    swapped = pl.pallas_call(
        functools.partial(kernel, ny, nz),
        out_shape=jax.ShapeDtypeStruct((cols, rows, width), BF16),
        in_specs=[pl.BlockSpec(memory_space=pl.ANY)] * 8,
        out_specs=pl.BlockSpec(memory_space=pltpu.VMEM),
        scratch_shapes=[
            pltpu.SMEM(token_mask.shape, jnp.int32),
            pltpu.VMEM(pair.shape, BF16),
            pltpu.VMEM((1, width), F32),
            pltpu.VMEM((1, width), F32),
            pltpu.VMEM(w_left.shape, BF16),
            pltpu.VMEM(w_right.shape, BF16),
            pltpu.VMEM(w_gate.shape, BF16),
            pltpu.VMEM(w_out.shape, BF16),
            dma((8,)),
            pltpu.VMEM((nt, rows * ny, width), F32),
            pltpu.VMEM((nt, rows * ny, width), BF16),
            pltpu.VMEM((nt, rows * ny, width), F32),
            pltpu.VMEM((4 * chans, width), BF16),
            pltpu.VMEM((ny, 2 * nz, lanes), BF16),
            pltpu.VMEM((ny, 2 * nz, third), BF16),
            pltpu.VMEM((ny, 2 * nz, lanes), BF16),
            pltpu.VMEM((ny, 2 * nz, third), BF16),
            pltpu.VMEM((nz, 2 * ny, lanes), BF16),
            pltpu.VMEM((nz, 2 * ny, third), BF16),
            pltpu.VMEM((nz, 2 * ny, lanes), BF16),
            pltpu.VMEM((nz, 2 * ny, third), BF16),
            pltpu.VMEM((nz, 2 * ny, lanes), BF16),
            pltpu.VMEM((nz, 2 * ny, third), BF16),
            pltpu.VMEM((2, nz, 2 * ny, lanes), BF16),
            pltpu.VMEM((2, nz, 2 * ny, third), BF16),
            pltpu.VMEM((ny, 2 * nz, lanes), BF16),
            pltpu.VMEM((ny, 2 * nz, third), BF16),
            pltpu.VMEM((ny, 2 * nz, lanes), BF16),
            pltpu.VMEM((ny, 2 * nz, third), BF16),
            pltpu.VMEM((2, ny, 2 * nz, lanes), BF16),
            pltpu.VMEM((2, ny, 2 * nz, third), BF16),
            pltpu.VMEM((nz, rows, lanes), F32),
            pltpu.VMEM((nz, cols, lanes), F32),
            pltpu.VMEM((nz, 2 * ny, lanes), BF16),
            pltpu.VMEM((nz, 2 * ny, lanes), BF16),
            pltpu.VMEM((ny, 2 * nz, lanes), BF16),
            pltpu.VMEM((ny, 2 * nz, lanes), BF16),
            pltpu.VMEM((nz, 2 * ny, third), BF16),
            pltpu.VMEM((nz, 2 * ny, third), BF16),
            pltpu.VMEM((ny, 2 * nz, third), BF16),
            pltpu.VMEM((ny, 2 * nz, third), BF16),
        ] + [dma((2,))] * 4 + [dma((2,)), dma((2, nz)), dma((2,)), dma((2, ny))] + [dma((2,))] * 4 + [dma, dma] + [dma((2,))] * 4,
        compiler_params=pltpu.CompilerParams(
            collective_id=0, has_side_effects=True, vmem_limit_bytes=64 * 1024 * 1024
        ),
    )(token_mask, pair, ln_gain.reshape(1, width), ln_bias.reshape(1, width), w_left, w_right, w_gate, w_out)
    return jnp.transpose(swapped, (1, 0, 2))


def solution(mesh):
    ny, nz = mesh.shape["row"] // 2, mesh.shape["col"] // 4
    placed = (P("row", "col", None), P(), P(), P(), P(), P(), P(), P())
    return jax.shard_map(
        functools.partial(per_device, ny, nz), mesh=mesh, in_specs=placed,
        out_specs=P("row", "col", None), check_vma=False,
    )
```

```python
import functools
import math

import jax
import jax.numpy as jnp
from jax import lax
from jax.experimental import pallas as pl
from jax.experimental.pallas import tpu as pltpu
from jax.sharding import PartitionSpec as P

F32 = jnp.float32
BF16 = jnp.bfloat16
MESH = pl.DeviceIdType.MESH


def one_hot(shape, source):
    row = lax.broadcasted_iota(jnp.int32, shape, 0)
    col = lax.broadcasted_iota(jnp.int32, shape, 1)
    return row, col, source(row)


def permutation(count, source):
    _, col, src = one_hot((count, count), source)
    return jnp.where(col == src, 1.0, 0.0).astype(BF16)


def swap_ends(a, b, c):
    return permutation(a * b * c, lambda o: (o % a) * (b * c) + ((o // a) % b) * c + o // (a * b))


def far_first(n):
    return sorted(range(1, n), key=lambda d: -min(d, n - d))


def nt_dot(x, y):
    return lax.dot_general(x, y, (((1,), (1,)), ((), ())), preferred_element_type=F32)


def tn_dot(x, y):
    return lax.dot_general(x, y, (((0,), (0,)), ((), ())), preferred_element_type=F32)


def nn_dot(x, y):
    return lax.dot_general(x, y, (((1,), (0,)), ((), ())), preferred_element_type=F32)


def exchange(parts, width):
    n = len(parts)
    total = n * width
    pos = lax.broadcasted_iota(jnp.int32, parts[0].shape, 1) // width
    rolled = [parts[0]] + [pltpu.roll(parts[y], y * width, 1) for y in range(1, n)]
    result = []
    for k in range(n):
        picked = rolled[0]
        for y in range(1, n):
            picked = jnp.where(pos == (k + y) % n, rolled[y], picked)
        result.append(picked if k == 0 else pltpu.roll(picked, total - k * width, 1))
    return result


def fold(block):
    third = block.shape[1] // 3
    a, b, c = (block[:, i * third:(i + 1) * third] for i in range(3))
    return jnp.concatenate(
        [jnp.concatenate([a, b], 0), jnp.concatenate([c, jnp.zeros_like(c)], 0)], 1
    )


def unfold(block):
    n, third = block.shape[0] // 2, block.shape[1] // 2
    return jnp.concatenate([block[:n, :third], block[n:, :third], block[:n, third:]], 1)


def kernel(
    ny, nz, tm_hbm, pair_hbm, gain_hbm, bias_hbm, wl_hbm, wr_hbm, wg_hbm, wo_hbm, out,
    tm, pair, gain, bias, w_left, w_right, w_gate, w_out, load, n32, normed, gate, wt,
    a1l, a1lf, b1l, b1lf, a1r, a1rf, b1r, b1rf, a2l, a2lf, b2l, b2lf, a2r, a2rf, b2r, b2rf, rx, rxf,
    pp, qq, sa, fa, ga, ha, sb, fb, gb, hb,
    s1l, r1l, s1r, r1r, s2l, r2l, s2r, r2r, sl, rl, sr, rr, sq, rq, s3, r3, s4, r4,
):
    rows, cols, width = pair.shape
    nt = cols // ny
    lanes = ny * rows
    chans = ny * nz
    loads = [
        pltpu.make_async_copy(src, dst, load.at[i])
        for i, (src, dst) in enumerate((
            (pair_hbm, pair), (wl_hbm, w_left), (wr_hbm, w_right), (tm_hbm, tm),
            (gain_hbm, gain), (bias_hbm, bias), (wg_hbm, w_gate), (wo_hbm, w_out),
        ))
    ]
    row, col = lax.axis_index("row"), lax.axis_index("col")
    y, xh = row // 2, row % 2
    z, xl, core = col // 4, (col // 2) % 2, col % 2
    same = xl == xh

    def at_y(d):
        return lax.rem(y + d, ny)

    def at_z(d):
        return lax.rem(z + d, nz)

    def dev_y(other):
        return (other * 2 + xh, col)

    def dev_z(other):
        return (row, other * 4 + xl * 2 + core)

    def dev_x(oh, ol):
        return (y * 2 + oh, z * 4 + ol * 2 + core)

    other_core = (row, z * 4 + xl * 2 + 1 - core)
    peers = [dev_y(at_y(d)) for d in far_first(ny)] + [dev_z(at_z(d)) for d in far_first(nz)]
    peers += [dev_x(xh, 1 - xl), dev_x(1 - xh, xl), dev_x(1 - xh, 1 - xl), other_core]
    barrier = pltpu.get_barrier_semaphore()
    for peer in peers:
        pl.semaphore_signal(barrier, inc=1, device_id=peer, device_id_type=MESH)

    for copy in loads:
        copy.start()

    def send(src, dst, send_sem, recv_sem, device):
        pltpu.make_async_remote_copy(
            src_ref=src, dst_ref=dst, send_sem=send_sem, recv_sem=recv_sem,
            device_id=device, device_id_type=MESH,
        ).start()

    def take(ref, sem):
        pltpu.make_async_copy(ref, ref, sem).wait()

    for copy in loads[1:]:
        copy.wait()

    _, c, r = one_hot((2 * chans, 2 * chans), lambda o: o)
    wt[0:2 * chans, :] = nt_dot(jnp.where(c == r, 1.0, 0.0).astype(BF16), w_left[...]).astype(BF16)
    _, c, r = one_hot(
        (2 * chans, 2 * chans), lambda o: (o // chans) * chans + (o % ny) * nz + (o % chans) // ny
    )
    wt[2 * chans:4 * chans, :] = nt_dot(jnp.where(c == r, 1.0, 0.0).astype(BF16), w_right[...]).astype(BF16)

    lane = lax.broadcasted_iota(jnp.int32, (1, lanes), 1)
    row_mask = jnp.zeros((1, lanes), F32)
    for i in range(rows):
        row_mask = jnp.where(lane % rows == i, tm[row * rows + i].astype(F32), row_mask)

    def mask_of(t):
        col_mask = jnp.zeros((1, lanes), F32)
        for k in range(ny):
            col_mask = jnp.where(lane // rows == k, tm[col * cols + t * ny + k].astype(F32), col_mask)
        return row_mask * col_mask

    def project(t):
        block = pair[:, t * ny:(t + 1) * ny, :].astype(F32)
        center = jnp.mean(block, axis=-1, keepdims=True)
        delta = block - center
        spread = jnp.mean(delta * delta, axis=-1, keepdims=True)
        value = delta * lax.rsqrt(spread + 1e-05) * gain[...].reshape(1, 1, width) + bias[...].reshape(1, 1, width)
        n32[t] = value.reshape(rows * ny, width)
        for k in range(ny):
            normed[t, k * rows:(k + 1) * rows, :] = n32[t, pl.ds(k, rows, stride=ny), :].astype(BF16)
        proj = nt_dot(wt[...], normed[t])
        mask = mask_of(t)
        sides = (proj[:2 * chans], proj[2 * chans:])
        return [jax.nn.sigmoid(side[:chans]) * side[chans:] * mask for side in sides]

    swap1 = swap_ends(ny, 2, nz)
    swap2 = swap_ends(ny, 1, nz)

    def send_first(left, left_land, right, right_land, part):
        for d in far_first(ny):
            to = at_y(d)
            send(left.at[to], left_land.at[y], s1l.at[part], r1l.at[part], dev_y(to))
        for d in far_first(nz):
            to = at_z(d)
            send(right.at[to], right_land.at[z], s1r.at[part], r1r.at[part], dev_z(to))
        left_land[y] = left[y]
        right_land[z] = right[z]

    loads[0].wait()
    left0, right0 = project(0)
    left1, right1 = project(1)
    pairs = lambda u, v, n: jnp.concatenate([u.reshape(n, -1, lanes), v.reshape(n, -1, lanes)], 1).astype(BF16)
    a1l[...] = pairs(left0, left1, ny)
    a1r[...] = pairs(right0, right1, nz)
    pl.semaphore_wait(barrier, len(peers))
    send_first(a1l, b1l, a1r, b1r, 0)
    left2, right2 = project(2)
    for k in range(ny):
        a1lf[k] = fold(left2[k * nz:(k + 1) * nz]).astype(BF16)
    for k in range(nz):
        a1rf[k] = fold(right2[k * ny:(k + 1) * ny]).astype(BF16)
    send_first(a1lf, b1lf, a1rf, b1rf, 1)

    def turn_right(land, part, out_buf, dst):
        take(land.at[pl.ds(0, nz - 1)], r1r.at[part])
        out_buf[...] = nn_dot(swap1, land[...].reshape(nz * 2 * ny, -1)).astype(BF16).reshape(out_buf.shape)
        for d in far_first(ny):
            to = at_y(d)
            send(out_buf.at[to], dst.at[y], s2r.at[part], r2r.at[part, y], dev_y(to))
        dst[y] = out_buf[y]

    def send_left(out_buf, dst, part):
        for d in far_first(nz):
            to = at_z(d)
            send(out_buf.at[to], dst.at[xl, z], s2l.at[part], r2l.at[part, z], dev_z(to))
        dst[xl, z] = out_buf[z]

    take(b1l.at[pl.ds(0, ny - 1)], r1l.at[0])
    parts = exchange([b1l[k].astype(F32) for k in range(ny)], rows)
    a2l[...] = nn_dot(swap1, jnp.concatenate(parts, 0).astype(BF16)).astype(BF16).reshape(a2l.shape)
    send_left(a2l, b2l, 0)
    turn_right(b1r, 0, a2r, b2r)
    take(b1lf.at[pl.ds(0, ny - 1)], r1l.at[1])
    parts = exchange([unfold(b1lf[k].astype(F32)) for k in range(ny)], rows)
    turned = nn_dot(swap2, jnp.concatenate(parts, 0).astype(BF16))
    for k in range(nz):
        a2lf[k] = fold(turned[k * ny:(k + 1) * ny]).astype(BF16)
    send_left(a2lf, b2lf, 1)
    turn_right(b1rf, 1, a2rf, b2rf)

    for t in range(nt):
        gate[t] = jax.nn.sigmoid(nn_dot(normed[t], w_gate[...]))

    def forward(left, right, right_dst, part):
        def forward_left(k):
            send(left.at[xl, k], left.at[xl, k], sl.at[part], rl.at[part], dev_x(xh, 1 - xl))

        def forward_right(k):
            send(right.at[k], right_dst.at[xl, k], sr.at[part], rr.at[part], dev_x(1 - xh, xh))

            @pl.when(jnp.logical_not(same))
            def _():
                send(right.at[k], right_dst.at[xl, k], sr.at[part], rr.at[part], dev_x(xh, xh))

        forward_right(y)
        forward_left(z)
        for d in reversed(far_first(ny)):
            k = at_y(d)
            take(right.at[k], r2r.at[part, k])
            forward_right(k)
            k = at_z(d)
            take(left.at[xl, k], r2l.at[part, k])
            forward_left(k)

        @pl.when(same)
        def _():
            right_dst[xl] = right[...]

    def gather_x(left, right_dst, part):
        take(left.at[0], rl.at[part])

        @pl.when(same)
        def _():
            take(right_dst.at[0], rr.at[part])

        @pl.when(jnp.logical_not(same))
        def _():
            take(right_dst, rr.at[part])

    forward(b2l, b2r, rx, 0)
    forward(b2lf, b2rf, rxf, 1)

    two = 2 * ny
    gather_x(b2l, rx, 0)
    panels = []
    for x in range(2):
        parts = exchange([rx[x, k].astype(F32) for k in range(ny)], rows)
        panels.append(nn_dot(swap1, jnp.concatenate(parts, 0).astype(BF16)).astype(BF16))
    total = tn_dot(jnp.concatenate(panels, 0), b2l[...].reshape(2 * nz * two, lanes))
    gather_x(b2lf, rxf, 1)
    panels = []
    for x in range(2):
        parts = exchange([unfold(rxf[x, k].astype(F32)) for k in range(ny)], rows)
        panels.append(nn_dot(swap2, jnp.concatenate(parts, 0).astype(BF16)).astype(BF16))
    lefts = [unfold(b2lf[x, k].astype(F32)) for x in range(2) for k in range(nz)]
    right, left = jnp.concatenate(panels, 0), jnp.concatenate(lefts, 0).astype(BF16)
    scale = 4.0 / math.sqrt(rows * 2 * ny)
    cut = lanes // 3
    ahead = max(1, cut // rows)
    groups = ((0, ahead, -(-ahead * rows // cut) * cut), (ahead, nz, lanes))

    done = 0
    for g, (low, high, until) in enumerate(groups):
        pp[done:until] = total[done:until] + tn_dot(right[:, done:until], left)
        done = until
        for k in range(low, high):
            send(pp.at[pl.ds(k * rows + (1 - core) * cols, cols)], qq.at[k], sq.at[g], rq.at[g], other_core)
    for g, (low, high, _) in enumerate(groups):
        take(qq.at[pl.ds(low, high - low)], rq.at[g])
        for k in range(low, high):
            tri = (pp[pl.ds(k * rows + core * cols, cols), :] + qq[k]) * scale
            sa[k] = tri[:two].astype(BF16)
            sb[k] = fold(tri[two:]).astype(BF16)

            @pl.when(z != k)
            def _():
                send(sa.at[k], fa.at[z], s3.at[0], r3.at[0], dev_z(k))
                send(sb.at[k], fb.at[z], s3.at[1], r3.at[1], dev_z(k))
    fa[z] = sa[z]
    fb[z] = sb[z]

    take(fa.at[pl.ds(0, nz - 1)], r3.at[0])
    turned = nn_dot(swap_ends(nz, 2, ny), fa[...].reshape(nz * two, lanes)).reshape(ny, 2 * nz, lanes)
    parts = exchange([turned[j] for j in range(ny)], rows)
    for k in range(ny):
        ga[k] = parts[k].astype(BF16)
    for d in far_first(ny):
        to = at_y(d)
        send(ga.at[to], ha.at[y], s4.at[0], r4.at[0], dev_y(to))
    ha[y] = ga[y]

    take(fb.at[pl.ds(0, nz - 1)], r3.at[1])
    flat = jnp.concatenate([unfold(fb[k].astype(F32)) for k in range(nz)], 0).astype(BF16)
    turned = nn_dot(swap_ends(nz, 1, ny), flat).reshape(ny, nz, lanes)
    parts = exchange([turned[j] for j in range(ny)], rows)
    for k in range(ny):
        gb[k] = fold(parts[k]).astype(BF16)
    for d in far_first(ny):
        to = at_y(d)
        send(gb.at[to], hb.at[y], s4.at[1], r4.at[1], dev_y(to))
    hb[y] = gb[y]

    def finish(t, block):
        mixed = tn_dot(block.reshape(chans, lanes).astype(BF16), w_out[...])
        out[t * ny:(t + 1) * ny] = (gate[t] * mixed).astype(BF16).reshape(ny, rows, width)

    take(ha.at[pl.ds(0, ny - 1)], r4.at[0])
    both = ha[...].astype(F32).reshape(ny, 2, nz, lanes)
    finish(0, both[:, 0])
    finish(1, both[:, 1])
    take(hb.at[pl.ds(0, ny - 1)], r4.at[1])
    finish(2, jnp.concatenate([unfold(hb[k].astype(F32)) for k in range(ny)], 0))

    for part, (first, second, land) in enumerate(((a1l, a2l, rx), (a1lf, a2lf, rxf))):
        take(first.at[pl.ds(0, ny - 1)], s1l.at[part])
        take(first.at[pl.ds(0, nz - 1)], s1r.at[part])
        take(second.at[pl.ds(0, nz - 1)], s2l.at[part])
        take(second.at[pl.ds(0, ny - 1)], s2r.at[part])
        take(land.at[0], sl.at[part])

        @pl.when(same)
        def _():
            take(land.at[0], sr.at[part])

        @pl.when(jnp.logical_not(same))
        def _():
            take(land, sr.at[part])
    for g, (low, high, _) in enumerate(groups):
        take(qq.at[pl.ds(low, high - low)], sq.at[g])
    take(sa.at[pl.ds(0, nz - 1)], s3.at[0])
    take(sb.at[pl.ds(0, nz - 1)], s3.at[1])
    take(ga.at[pl.ds(0, ny - 1)], s4.at[0])
    take(gb.at[pl.ds(0, ny - 1)], s4.at[1])


def per_device(ny, nz, pair, token_mask, ln_gain, ln_bias, w_left, w_right, w_gate, w_out):
    rows, cols, width = pair.shape
    lanes = ny * rows
    nt = cols // ny
    chans = ny * nz
    third = 2 * lanes // 3
    dma = pltpu.SemaphoreType.DMA
    swapped = pl.pallas_call(
        functools.partial(kernel, ny, nz),
        out_shape=pltpu.VMEM((cols, rows, width), BF16),
        in_specs=[pl.BlockSpec(memory_space=pl.ANY)] * 8,
        out_specs=pl.BlockSpec(memory_space=pltpu.VMEM),
        scratch_shapes=[
            pltpu.SMEM(token_mask.shape, jnp.int32),
            pltpu.VMEM(pair.shape, BF16),
            pltpu.VMEM((1, width), F32),
            pltpu.VMEM((1, width), F32),
            pltpu.VMEM(w_left.shape, BF16),
            pltpu.VMEM(w_right.shape, BF16),
            pltpu.VMEM(w_gate.shape, BF16),
            pltpu.VMEM(w_out.shape, BF16),
            dma((8,)),
            pltpu.VMEM((nt, rows * ny, width), F32),
            pltpu.VMEM((nt, rows * ny, width), BF16),
            pltpu.VMEM((nt, rows * ny, width), F32),
            pltpu.VMEM((4 * chans, width), BF16),
            pltpu.VMEM((ny, 2 * nz, lanes), BF16),
            pltpu.VMEM((ny, 2 * nz, third), BF16),
            pltpu.VMEM((ny, 2 * nz, lanes), BF16),
            pltpu.VMEM((ny, 2 * nz, third), BF16),
            pltpu.VMEM((nz, 2 * ny, lanes), BF16),
            pltpu.VMEM((nz, 2 * ny, third), BF16),
            pltpu.VMEM((nz, 2 * ny, lanes), BF16),
            pltpu.VMEM((nz, 2 * ny, third), BF16),
            pltpu.VMEM((nz, 2 * ny, lanes), BF16),
            pltpu.VMEM((nz, 2 * ny, third), BF16),
            pltpu.VMEM((2, nz, 2 * ny, lanes), BF16),
            pltpu.VMEM((2, nz, 2 * ny, third), BF16),
            pltpu.VMEM((ny, 2 * nz, lanes), BF16),
            pltpu.VMEM((ny, 2 * nz, third), BF16),
            pltpu.VMEM((ny, 2 * nz, lanes), BF16),
            pltpu.VMEM((ny, 2 * nz, third), BF16),
            pltpu.VMEM((2, ny, 2 * nz, lanes), BF16),
            pltpu.VMEM((2, ny, 2 * nz, third), BF16),
            pltpu.VMEM((lanes, lanes), F32),
            pltpu.VMEM((nz, cols, lanes), F32),
            pltpu.VMEM((nz, 2 * ny, lanes), BF16),
            pltpu.VMEM((nz, 2 * ny, lanes), BF16),
            pltpu.VMEM((ny, 2 * nz, lanes), BF16),
            pltpu.VMEM((ny, 2 * nz, lanes), BF16),
            pltpu.VMEM((nz, 2 * ny, third), BF16),
            pltpu.VMEM((nz, 2 * ny, third), BF16),
            pltpu.VMEM((ny, 2 * nz, third), BF16),
            pltpu.VMEM((ny, 2 * nz, third), BF16),
        ] + [dma((2,))] * 4 + [dma((2,)), dma((2, nz)), dma((2,)), dma((2, ny))] + [dma((2,))] * 10,
        compiler_params=pltpu.CompilerParams(
            collective_id=0, has_side_effects=True, vmem_limit_bytes=60 * 1024 * 1024
        ),
    )(token_mask, pair, ln_gain.reshape(1, width), ln_bias.reshape(1, width), w_left, w_right, w_gate, w_out)
    return jnp.transpose(swapped, (1, 0, 2))


def solution(mesh):
    ny, nz = mesh.shape["row"] // 2, mesh.shape["col"] // 4
    placed = (P("row", "col", None), P(), P(), P(), P(), P(), P(), P())
    return jax.shard_map(
        functools.partial(per_device, ny, nz), mesh=mesh, in_specs=placed,
        out_specs=P("row", "col", None), check_vma=False,
    )
```

```python
import functools
import math

import jax
import jax.numpy as jnp
from jax import lax
from jax.experimental import pallas as pl
from jax.experimental.pallas import tpu as pltpu
from jax.sharding import PartitionSpec as P

F32 = jnp.float32
BF16 = jnp.bfloat16
MESH = pl.DeviceIdType.MESH


def one_hot(shape, source):
    row = lax.broadcasted_iota(jnp.int32, shape, 0)
    col = lax.broadcasted_iota(jnp.int32, shape, 1)
    return row, col, source(row)


def permutation(count, source):
    _, col, src = one_hot((count, count), source)
    return jnp.where(col == src, 1.0, 0.0).astype(BF16)


def swap_ends(a, b, c):
    return permutation(a * b * c, lambda o: (o % a) * (b * c) + ((o // a) % b) * c + o // (a * b))


def far_first(n):
    return sorted(range(1, n), key=lambda d: -min(d, n - d))


def nt_dot(x, y):
    return lax.dot_general(x, y, (((1,), (1,)), ((), ())), preferred_element_type=F32)


def tn_dot(x, y):
    return lax.dot_general(x, y, (((0,), (0,)), ((), ())), preferred_element_type=F32)


def nn_dot(x, y):
    return lax.dot_general(x, y, (((1,), (0,)), ((), ())), preferred_element_type=F32)


def spread(parts, width):
    return [pltpu.roll(part, y * width, 1) if y else part for y, part in enumerate(parts)]


def pick(rolled, width, k, keep=None):
    total = rolled[0].shape[1]
    n = total // width
    pos = lax.broadcasted_iota(jnp.int32, rolled[0].shape, 1) // width
    picked = rolled[0]
    for y, part in list(enumerate(rolled))[1:]:
        picked = jnp.where(pos == (k + y) % n, part, picked)
    return (pltpu.roll(picked, total - k * width, 1) if k else picked)[:, :keep]


def exchange(parts, width, keep=None):
    rolled = spread(parts, width)
    return [pick(rolled, width, k, keep) for k in range(parts[0].shape[1] // width)]


def fold(block):
    third = block.shape[1] // 3
    a, b, c = (block[:, i * third:(i + 1) * third] for i in range(3))
    return jnp.concatenate(
        [jnp.concatenate([a, b], 0), jnp.concatenate([c, jnp.zeros_like(c)], 0)], 1
    )


def unfold(block):
    n, third = block.shape[0] // 2, block.shape[1] // 2
    return jnp.concatenate([block[:n, :third], block[n:, :third], block[:n, third:]], 1)


def kernel(
    ny, nz, tm_hbm, pair_hbm, gain_hbm, bias_hbm, wl_hbm, wr_hbm, wg_hbm, wo_hbm, out,
    tm, pair, gain, bias, w_left, w_right, w_gate, w_out, load, n32, normed, gate, wt,
    a1l, a1lf, b1l, b1lf, a1r, a1rf, b1r, b1rf, a2l, a2lf, b2l, b2lf, a2r, a2rf, b2r, b2rf, rx, rxf,
    pp, qq, sa, fa, ga, ha, sb, fb, gb, hb,
    s1l, r1l, s1r, r1r, s2l, r2l, s2r, r2r, sl, rl, sr, rr, sq, rq, s3, r3, s4, r4,
):
    rows, cols, width = pair.shape
    nt = cols // ny
    lanes = ny * rows
    chans = ny * nz
    loads = [
        pltpu.make_async_copy(src, dst, load.at[i])
        for i, (src, dst) in enumerate((
            (pair_hbm, pair), (wl_hbm, w_left), (wr_hbm, w_right), (tm_hbm, tm),
            (gain_hbm, gain), (bias_hbm, bias), (wg_hbm, w_gate), (wo_hbm, w_out),
        ))
    ]
    row, col = lax.axis_index("row"), lax.axis_index("col")
    y, xh = row // 2, row % 2
    z, xl, core = col // 4, (col // 2) % 2, col % 2
    same = xl == xh

    def at_y(d):
        return lax.rem(y + d, ny)

    def at_z(d):
        return lax.rem(z + d, nz)

    def dev_y(other):
        return (other * 2 + xh, col)

    def dev_z(other):
        return (row, other * 4 + xl * 2 + core)

    def dev_x(oh, ol):
        return (y * 2 + oh, z * 4 + ol * 2 + core)

    other_core = (row, z * 4 + xl * 2 + 1 - core)
    peers = [dev_y(at_y(d)) for d in far_first(ny)] + [dev_z(at_z(d)) for d in far_first(nz)]
    peers += [dev_x(xh, 1 - xl), dev_x(1 - xh, xl), dev_x(1 - xh, 1 - xl), other_core]
    barrier = pltpu.get_barrier_semaphore()
    for peer in peers:
        pl.semaphore_signal(barrier, inc=1, device_id=peer, device_id_type=MESH)

    for copy in loads:
        copy.start()

    def send(src, dst, send_sem, recv_sem, device):
        pltpu.make_async_remote_copy(
            src_ref=src, dst_ref=dst, send_sem=send_sem, recv_sem=recv_sem,
            device_id=device, device_id_type=MESH,
        ).start()

    def take(ref, sem):
        pltpu.make_async_copy(ref, ref, sem).wait()

    for copy in loads[1:]:
        copy.wait()

    _, c, r = one_hot((2 * chans, 2 * chans), lambda o: o)
    wt[0:2 * chans, :] = nt_dot(jnp.where(c == r, 1.0, 0.0).astype(BF16), w_left[...]).astype(BF16)
    _, c, r = one_hot(
        (2 * chans, 2 * chans), lambda o: (o // chans) * chans + (o % ny) * nz + (o % chans) // ny
    )
    wt[2 * chans:4 * chans, :] = nt_dot(jnp.where(c == r, 1.0, 0.0).astype(BF16), w_right[...]).astype(BF16)

    lane = lax.broadcasted_iota(jnp.int32, (1, lanes), 1)
    row_mask = jnp.zeros((1, lanes), F32)
    for i in range(rows):
        row_mask = jnp.where(lane % rows == i, tm[row * rows + i].astype(F32), row_mask)

    def mask_of(t):
        col_mask = jnp.zeros((1, lanes), F32)
        for k in range(ny):
            col_mask = jnp.where(lane // rows == k, tm[col * cols + t * ny + k].astype(F32), col_mask)
        return row_mask * col_mask

    def project(t):
        block = pair[:, t * ny:(t + 1) * ny, :].astype(F32)
        center = jnp.mean(block, axis=-1, keepdims=True)
        delta = block - center
        spread = jnp.mean(delta * delta, axis=-1, keepdims=True)
        value = delta * lax.rsqrt(spread + 1e-05) * gain[...].reshape(1, 1, width) + bias[...].reshape(1, 1, width)
        n32[t] = value.reshape(rows * ny, width)
        for k in range(ny):
            normed[t, k * rows:(k + 1) * rows, :] = n32[t, pl.ds(k, rows, stride=ny), :].astype(BF16)
        proj = nt_dot(wt[...], normed[t])
        mask = mask_of(t)
        sides = (proj[:2 * chans], proj[2 * chans:])
        return [jax.nn.sigmoid(side[:chans]) * side[chans:] * mask for side in sides]

    swap1 = swap_ends(ny, 2, nz)
    swap2 = swap_ends(ny, 1, nz)

    def send_first(left, left_land, right, right_land, part):
        for d in far_first(ny):
            to = at_y(d)
            send(left.at[to], left_land.at[y], s1l.at[part], r1l.at[part], dev_y(to))
        for d in far_first(nz):
            to = at_z(d)
            send(right.at[to], right_land.at[z], s1r.at[part], r1r.at[part], dev_z(to))
        left_land[y] = left[y]
        right_land[z] = right[z]

    loads[0].wait()
    left0, right0 = project(0)
    left1, right1 = project(1)
    pairs = lambda u, v, n: jnp.concatenate([u.reshape(n, -1, lanes), v.reshape(n, -1, lanes)], 1).astype(BF16)
    a1l[...] = pairs(left0, left1, ny)
    a1r[...] = pairs(right0, right1, nz)
    pl.semaphore_wait(barrier, len(peers))
    send_first(a1l, b1l, a1r, b1r, 0)
    left2, right2 = project(2)
    for k in range(ny):
        a1lf[k] = fold(left2[k * nz:(k + 1) * nz]).astype(BF16)
    for k in range(nz):
        a1rf[k] = fold(right2[k * ny:(k + 1) * ny]).astype(BF16)
    send_first(a1lf, b1lf, a1rf, b1rf, 1)

    def turn_right(land, part, out_buf, dst):
        take(land.at[pl.ds(0, nz - 1)], r1r.at[part])
        out_buf[...] = nn_dot(swap1, land[...].reshape(nz * 2 * ny, -1)).astype(BF16).reshape(out_buf.shape)
        for d in far_first(ny):
            to = at_y(d)
            send(out_buf.at[to], dst.at[y], s2r.at[part], r2r.at[part, y], dev_y(to))
        dst[y] = out_buf[y]

    def send_left(out_buf, dst, part):
        for d in far_first(nz):
            to = at_z(d)
            send(out_buf.at[to], dst.at[xl, z], s2l.at[part], r2l.at[part, z], dev_z(to))
        dst[xl, z] = out_buf[z]

    take(b1l.at[pl.ds(0, ny - 1)], r1l.at[0])
    parts = exchange([b1l[k].astype(F32) for k in range(ny)], rows)
    a2l[...] = nn_dot(swap1, jnp.concatenate(parts, 0).astype(BF16)).astype(BF16).reshape(a2l.shape)
    send_left(a2l, b2l, 0)
    turn_right(b1r, 0, a2r, b2r)
    take(b1lf.at[pl.ds(0, ny - 1)], r1l.at[1])
    parts = exchange([unfold(b1lf[k].astype(F32)) for k in range(ny)], rows)
    turned = nn_dot(swap2, jnp.concatenate(parts, 0).astype(BF16))
    for k in range(nz):
        a2lf[k] = fold(turned[k * ny:(k + 1) * ny]).astype(BF16)
    send_left(a2lf, b2lf, 1)
    turn_right(b1rf, 1, a2rf, b2rf)

    for t in range(nt):
        gate[t] = jax.nn.sigmoid(nn_dot(normed[t], w_gate[...]))

    ahead = max(1, lanes // (3 * rows))
    cut = -(-ahead * rows * 3 // lanes) * (lanes // 3)
    groups = ((0, ahead), (ahead, nz))

    def forward_left(left, part, k):
        send(left.at[xl, k], left.at[xl, k], sl.at[part], rl.at[part], dev_x(xh, 1 - xl))

    def forward_right(right, dst, part, g):
        low, high = groups[g]
        for k in range(low, high):
            @pl.when(y != k)
            def _():
                take(right.at[k], r2r.at[part, k])

            send(right.at[k], dst.at[xl, k], sr.at[part, g], rr.at[part, g], dev_x(1 - xh, xh))

            @pl.when(jnp.logical_not(same))
            def _():
                send(right.at[k], dst.at[xl, k], sr.at[part, g], rr.at[part, g], dev_x(xh, xh))

        @pl.when(same)
        def _():
            dst[xl, low:high] = right[low:high]

    for part, (left, right, dst) in enumerate(((b2l, b2r, rx), (b2lf, b2rf, rxf))):
        forward_left(left, part, z)
        order = far_first(nz)[::-1]
        for place, d in enumerate(order):
            if place == len(order) // 2:
                forward_right(right, dst, part, 0)
            k = at_z(d)
            take(left.at[xl, k], r2l.at[part, k])
            forward_left(left, part, k)
    forward_right(b2r, rx, 0, 1)
    forward_right(b2rf, rxf, 1, 1)

    two = 2 * ny

    def take_right(dst, part, g, sem):
        low, high = groups[g]

        @pl.when(same)
        def _():
            take(dst.at[0, pl.ds(low, high - low)], sem.at[part, g])

        @pl.when(jnp.logical_not(same))
        def _():
            take(dst.at[:, pl.ds(low, high - low)], sem.at[part, g])

    def panel(g):
        count, keep = (ahead, cut) if g == 0 else (ny, lanes)

        def stack(parts, swap):
            return nn_dot(swap, jnp.concatenate(exchange(parts, rows, keep), 0).astype(BF16)).astype(BF16)

        return (
            lambda: jnp.concatenate([stack([rx[x, k].astype(F32) for k in range(count)], swap1) for x in range(2)], 0),
            lambda: jnp.concatenate(
                [stack([unfold(rxf[x, k].astype(F32)) for k in range(count)], swap2) for x in range(2)], 0
            ),
        )

    scale = 4.0 / math.sqrt(rows * 2 * ny)
    for g, (low, high) in enumerate(groups):
        if g == 0:
            take(b2l.at[0], rl.at[0])
        take_right(rx, 0, g, rr)
        panel_a, panel_b = panel(g)
        total = tn_dot(panel_a(), b2l[...].reshape(2 * nz * two, lanes))
        if g == 0:
            take(b2lf.at[0], rl.at[1])
            lefts = [unfold(b2lf[x, k].astype(F32)) for x in range(2) for k in range(nz)]
            left_b = jnp.concatenate(lefts, 0).astype(BF16)
        take_right(rxf, 1, g, rr)
        total = total + tn_dot(panel_b(), left_b)
        pp[low * rows:high * rows] = total[low * rows:high * rows]
        for k in range(low, high):
            send(pp.at[pl.ds(k * rows + (1 - core) * cols, cols)], qq.at[k], sq.at[g], rq.at[g], other_core)
        take(qq.at[pl.ds(low, high - low)], rq.at[g])
        for k in range(low, high):
            tri = (pp[pl.ds(k * rows + core * cols, cols), :] + qq[k]) * scale
            sa[k] = tri[:two].astype(BF16)
            sb[k] = fold(tri[two:]).astype(BF16)

            @pl.when(z != k)
            def _():
                send(sa.at[k], fa.at[z], s3.at[0], r3.at[0], dev_z(k))
                send(sb.at[k], fb.at[z], s3.at[1], r3.at[1], dev_z(k))
    fa[z] = sa[z]
    fb[z] = sb[z]

    take(fa.at[pl.ds(0, nz - 1)], r3.at[0])
    turned = nn_dot(swap_ends(nz, 2, ny), fa[...].reshape(nz * two, lanes)).reshape(ny, 2 * nz, lanes)
    rolled_a = spread([turned[j] for j in range(ny)], rows)
    take(fb.at[pl.ds(0, nz - 1)], r3.at[1])
    flat = jnp.concatenate([unfold(fb[k].astype(F32)) for k in range(nz)], 0).astype(BF16)
    turned = nn_dot(swap_ends(nz, 1, ny), flat).reshape(ny, nz, lanes)
    rolled_b = spread([turned[j] for j in range(ny)], rows)
    for k in sorted(range(ny), key=lambda k: min(k, ny - k + 1.6)):
        ga[k] = pick(rolled_a, rows, k).astype(BF16)
        gb[k] = fold(pick(rolled_b, rows, k)).astype(BF16)

        @pl.when(y != k)
        def _():
            send(ga.at[k], ha.at[y], s4.at[0], r4.at[0], dev_y(k))
            send(gb.at[k], hb.at[y], s4.at[1], r4.at[1], dev_y(k))
    ha[y] = ga[y]
    hb[y] = gb[y]

    def finish(t, block):
        mixed = tn_dot(block.reshape(chans, lanes).astype(BF16), w_out[...])
        out[t * ny:(t + 1) * ny] = (gate[t] * mixed).astype(BF16).reshape(ny, rows, width)

    take(ha.at[pl.ds(0, ny - 1)], r4.at[0])
    both = ha[...].astype(F32).reshape(ny, 2, nz, lanes)
    finish(0, both[:, 0])
    finish(1, both[:, 1])
    take(hb.at[pl.ds(0, ny - 1)], r4.at[1])
    finish(2, jnp.concatenate([unfold(hb[k].astype(F32)) for k in range(ny)], 0))

    for part, (first, second, land) in enumerate(((a1l, a2l, rx), (a1lf, a2lf, rxf))):
        take(first.at[pl.ds(0, ny - 1)], s1l.at[part])
        take(first.at[pl.ds(0, nz - 1)], s1r.at[part])
        take(second.at[pl.ds(0, nz - 1)], s2l.at[part])
        take(second.at[pl.ds(0, ny - 1)], s2r.at[part])
        take(land.at[0], sl.at[part])

        for g in range(2):
            take_right(land, part, g, sr)
    for g, (low, high) in enumerate(groups):
        take(qq.at[pl.ds(low, high - low)], sq.at[g])
    take(sa.at[pl.ds(0, nz - 1)], s3.at[0])
    take(sb.at[pl.ds(0, nz - 1)], s3.at[1])
    take(ga.at[pl.ds(0, ny - 1)], s4.at[0])
    take(gb.at[pl.ds(0, ny - 1)], s4.at[1])


def per_device(ny, nz, pair, token_mask, ln_gain, ln_bias, w_left, w_right, w_gate, w_out):
    rows, cols, width = pair.shape
    lanes = ny * rows
    nt = cols // ny
    chans = ny * nz
    third = 2 * lanes // 3
    dma = pltpu.SemaphoreType.DMA
    swapped = pl.pallas_call(
        functools.partial(kernel, ny, nz),
        out_shape=pltpu.VMEM((cols, rows, width), BF16),
        in_specs=[pl.BlockSpec(memory_space=pl.ANY)] * 8,
        out_specs=pl.BlockSpec(memory_space=pltpu.VMEM),
        scratch_shapes=[
            pltpu.SMEM(token_mask.shape, jnp.int32),
            pltpu.VMEM(pair.shape, BF16),
            pltpu.VMEM((1, width), F32),
            pltpu.VMEM((1, width), F32),
            pltpu.VMEM(w_left.shape, BF16),
            pltpu.VMEM(w_right.shape, BF16),
            pltpu.VMEM(w_gate.shape, BF16),
            pltpu.VMEM(w_out.shape, BF16),
            dma((8,)),
            pltpu.VMEM((nt, rows * ny, width), F32),
            pltpu.VMEM((nt, rows * ny, width), BF16),
            pltpu.VMEM((nt, rows * ny, width), F32),
            pltpu.VMEM((4 * chans, width), BF16),
            pltpu.VMEM((ny, 2 * nz, lanes), BF16),
            pltpu.VMEM((ny, 2 * nz, third), BF16),
            pltpu.VMEM((ny, 2 * nz, lanes), BF16),
            pltpu.VMEM((ny, 2 * nz, third), BF16),
            pltpu.VMEM((nz, 2 * ny, lanes), BF16),
            pltpu.VMEM((nz, 2 * ny, third), BF16),
            pltpu.VMEM((nz, 2 * ny, lanes), BF16),
            pltpu.VMEM((nz, 2 * ny, third), BF16),
            pltpu.VMEM((nz, 2 * ny, lanes), BF16),
            pltpu.VMEM((nz, 2 * ny, third), BF16),
            pltpu.VMEM((2, nz, 2 * ny, lanes), BF16),
            pltpu.VMEM((2, nz, 2 * ny, third), BF16),
            pltpu.VMEM((ny, 2 * nz, lanes), BF16),
            pltpu.VMEM((ny, 2 * nz, third), BF16),
            pltpu.VMEM((ny, 2 * nz, lanes), BF16),
            pltpu.VMEM((ny, 2 * nz, third), BF16),
            pltpu.VMEM((2, ny, 2 * nz, lanes), BF16),
            pltpu.VMEM((2, ny, 2 * nz, third), BF16),
            pltpu.VMEM((lanes, lanes), F32),
            pltpu.VMEM((nz, cols, lanes), F32),
            pltpu.VMEM((nz, 2 * ny, lanes), BF16),
            pltpu.VMEM((nz, 2 * ny, lanes), BF16),
            pltpu.VMEM((ny, 2 * nz, lanes), BF16),
            pltpu.VMEM((ny, 2 * nz, lanes), BF16),
            pltpu.VMEM((nz, 2 * ny, third), BF16),
            pltpu.VMEM((nz, 2 * ny, third), BF16),
            pltpu.VMEM((ny, 2 * nz, third), BF16),
            pltpu.VMEM((ny, 2 * nz, third), BF16),
        ] + [dma((2,))] * 4 + [dma((2,)), dma((2, nz)), dma((2,)), dma((2, ny))] + [dma((2,))] * 2 + [dma((2, 2))] * 2 + [dma((2,))] * 6,
        compiler_params=pltpu.CompilerParams(
            collective_id=0, has_side_effects=True, vmem_limit_bytes=60 * 1024 * 1024
        ),
    )(token_mask, pair, ln_gain.reshape(1, width), ln_bias.reshape(1, width), w_left, w_right, w_gate, w_out)
    return jnp.transpose(swapped, (1, 0, 2))


def solution(mesh):
    ny, nz = mesh.shape["row"] // 2, mesh.shape["col"] // 4
    placed = (P("row", "col", None), P(), P(), P(), P(), P(), P(), P())
    return jax.shard_map(
        functools.partial(per_device, ny, nz), mesh=mesh, in_specs=placed,
        out_specs=P("row", "col", None), check_vma=False,
    )
```

```python
import functools
import math

import jax
import jax.numpy as jnp
from jax import lax
from jax.experimental import pallas as pl
from jax.experimental.pallas import tpu as pltpu
from jax.sharding import PartitionSpec as P

F32 = jnp.float32
BF16 = jnp.bfloat16
MESH = pl.DeviceIdType.MESH


def one_hot(shape, source):
    row = lax.broadcasted_iota(jnp.int32, shape, 0)
    col = lax.broadcasted_iota(jnp.int32, shape, 1)
    return row, col, source(row)


def permutation(count, source):
    _, col, src = one_hot((count, count), source)
    return jnp.where(col == src, 1.0, 0.0).astype(BF16)


def swap_ends(a, b, c):
    return permutation(a * b * c, lambda o: (o % a) * (b * c) + ((o // a) % b) * c + o // (a * b))


def far_first(n):
    return sorted(range(1, n), key=lambda d: -min(d, n - d))


def nt_dot(x, y):
    return lax.dot_general(x, y, (((1,), (1,)), ((), ())), preferred_element_type=F32)


def tn_dot(x, y):
    return lax.dot_general(x, y, (((0,), (0,)), ((), ())), preferred_element_type=F32)


def nn_dot(x, y):
    return lax.dot_general(x, y, (((1,), (0,)), ((), ())), preferred_element_type=F32)


def spread(parts, width):
    return [pltpu.roll(part, y * width, 1) if y else part for y, part in enumerate(parts)]


def pick(rolled, width, k, keep=None):
    total = rolled[0].shape[1]
    n = total // width
    pos = lax.broadcasted_iota(jnp.int32, rolled[0].shape, 1) // width
    picked = rolled[0]
    for y, part in list(enumerate(rolled))[1:]:
        picked = jnp.where(pos == (k + y) % n, part, picked)
    return (pltpu.roll(picked, total - k * width, 1) if k else picked)[:, :keep]


def exchange(parts, width, keep=None):
    rolled = spread(parts, width)
    return [pick(rolled, width, k, keep) for k in range(parts[0].shape[1] // width)]


def fold(block):
    third = block.shape[1] // 3
    a, b, c = (block[:, i * third:(i + 1) * third] for i in range(3))
    return jnp.concatenate(
        [jnp.concatenate([a, b], 0), jnp.concatenate([c, jnp.zeros_like(c)], 0)], 1
    )


def unfold(block):
    n, third = block.shape[0] // 2, block.shape[1] // 2
    return jnp.concatenate([block[:n, :third], block[n:, :third], block[:n, third:]], 1)


def kernel(
    ny, nz, tm_hbm, pair_hbm, gain_hbm, bias_hbm, wl_hbm, wr_hbm, wg_hbm, wo_hbm, out,
    tm, pair, gain, bias, w_left, w_right, w_gate, w_out, load, n32, normed, gate, wt,
    a1l, a1lf, b1l, b1lf, a1r, a1rf, b1r, b1rf, a2l, a2lf, b2l, b2lf, a2r, a2rf, b2r, b2rf, rx, rxf,
    pp, qq, sc, land, f32,
    s1l, r1l, s1r, r1r, s2l, r2l, s2r, r2r, sl, rl, sr, rr, sq, rq, s3, r3,
):
    rows, cols, width = pair.shape
    nt = cols // ny
    lanes = ny * rows
    chans = ny * nz
    loads = [
        pltpu.make_async_copy(src, dst, load.at[i])
        for i, (src, dst) in enumerate((
            (pair_hbm, pair), (wl_hbm, w_left), (wr_hbm, w_right), (tm_hbm, tm),
            (gain_hbm, gain), (bias_hbm, bias), (wg_hbm, w_gate), (wo_hbm, w_out),
        ))
    ]
    row, col = lax.axis_index("row"), lax.axis_index("col")
    y, xh = row // 2, row % 2
    z, xl, core = col // 4, (col // 2) % 2, col % 2
    same = xl == xh

    def at_y(d):
        return lax.rem(y + d, ny)

    def at_z(d):
        return lax.rem(z + d, nz)

    def dev_y(other):
        return (other * 2 + xh, col)

    def dev_z(other):
        return (row, other * 4 + xl * 2 + core)

    def dev_x(oh, ol):
        return (y * 2 + oh, z * 4 + ol * 2 + core)

    other_core = (row, z * 4 + xl * 2 + 1 - core)
    peers = [dev_y(at_y(d)) for d in far_first(ny)] + [dev_z(at_z(d)) for d in far_first(nz)]
    peers += [dev_x(xh, 1 - xl), dev_x(1 - xh, xl), dev_x(1 - xh, 1 - xl), other_core]
    barrier = pltpu.get_barrier_semaphore()
    for peer in peers:
        pl.semaphore_signal(barrier, inc=1, device_id=peer, device_id_type=MESH)

    for copy in loads:
        copy.start()

    def send(src, dst, send_sem, recv_sem, device):
        pltpu.make_async_remote_copy(
            src_ref=src, dst_ref=dst, send_sem=send_sem, recv_sem=recv_sem,
            device_id=device, device_id_type=MESH,
        ).start()

    def take(ref, sem):
        pltpu.make_async_copy(ref, ref, sem).wait()

    for copy in loads[1:]:
        copy.wait()

    _, c, r = one_hot((2 * chans, 2 * chans), lambda o: o)
    wt[0:2 * chans, :] = nt_dot(jnp.where(c == r, 1.0, 0.0).astype(BF16), w_left[...]).astype(BF16)
    _, c, r = one_hot(
        (2 * chans, 2 * chans), lambda o: (o // chans) * chans + (o % ny) * nz + (o % chans) // ny
    )
    wt[2 * chans:4 * chans, :] = nt_dot(jnp.where(c == r, 1.0, 0.0).astype(BF16), w_right[...]).astype(BF16)

    lane = lax.broadcasted_iota(jnp.int32, (1, lanes), 1)
    row_mask = jnp.zeros((1, lanes), F32)
    for i in range(rows):
        row_mask = jnp.where(lane % rows == i, tm[row * rows + i].astype(F32), row_mask)

    def mask_of(t):
        col_mask = jnp.zeros((1, lanes), F32)
        for k in range(ny):
            col_mask = jnp.where(lane // rows == k, tm[col * cols + t * ny + k].astype(F32), col_mask)
        return row_mask * col_mask

    def project(t):
        block = pair[:, t * ny:(t + 1) * ny, :].astype(F32)
        center = jnp.mean(block, axis=-1, keepdims=True)
        delta = block - center
        spread = jnp.mean(delta * delta, axis=-1, keepdims=True)
        value = delta * lax.rsqrt(spread + 1e-05) * gain[...].reshape(1, 1, width) + bias[...].reshape(1, 1, width)
        n32[t] = value.reshape(rows * ny, width)
        for k in range(ny):
            normed[t, k * rows:(k + 1) * rows, :] = n32[t, pl.ds(k, rows, stride=ny), :].astype(BF16)
        proj = nt_dot(wt[...], normed[t])
        mask = mask_of(t)
        sides = (proj[:2 * chans], proj[2 * chans:])
        return [jax.nn.sigmoid(side[:chans]) * side[chans:] * mask for side in sides]

    swap1 = swap_ends(ny, 2, nz)
    swap2 = swap_ends(ny, 1, nz)

    def send_first(left, left_land, right, right_land, part):
        for d in far_first(ny):
            to = at_y(d)
            send(left.at[to], left_land.at[y], s1l.at[part], r1l.at[part], dev_y(to))
        for d in far_first(nz):
            to = at_z(d)
            send(right.at[to], right_land.at[z], s1r.at[part], r1r.at[part], dev_z(to))
        left_land[y] = left[y]
        right_land[z] = right[z]

    loads[0].wait()
    left0, right0 = project(0)
    left1, right1 = project(1)
    pairs = lambda u, v, n: jnp.concatenate([u.reshape(n, -1, lanes), v.reshape(n, -1, lanes)], 1).astype(BF16)
    a1l[...] = pairs(left0, left1, ny)
    a1r[...] = pairs(right0, right1, nz)
    pl.semaphore_wait(barrier, len(peers))
    send_first(a1l, b1l, a1r, b1r, 0)
    left2, right2 = project(2)
    for k in range(ny):
        a1lf[k] = fold(left2[k * nz:(k + 1) * nz]).astype(BF16)
    for k in range(nz):
        a1rf[k] = fold(right2[k * ny:(k + 1) * ny]).astype(BF16)
    send_first(a1lf, b1lf, a1rf, b1rf, 1)

    def turn_right(land, part, out_buf, dst):
        take(land.at[pl.ds(0, nz - 1)], r1r.at[part])
        out_buf[...] = nn_dot(swap1, land[...].reshape(nz * 2 * ny, -1)).astype(BF16).reshape(out_buf.shape)
        for d in far_first(ny):
            to = at_y(d)
            send(out_buf.at[to], dst.at[y], s2r.at[part], r2r.at[part, y], dev_y(to))
        dst[y] = out_buf[y]

    def send_left(out_buf, dst, part):
        for d in far_first(nz):
            to = at_z(d)
            send(out_buf.at[to], dst.at[xl, z], s2l.at[part], r2l.at[part, z], dev_z(to))
        dst[xl, z] = out_buf[z]

    take(b1l.at[pl.ds(0, ny - 1)], r1l.at[0])
    parts = exchange([b1l[k].astype(F32) for k in range(ny)], rows)
    a2l[...] = nn_dot(swap1, jnp.concatenate(parts, 0).astype(BF16)).astype(BF16).reshape(a2l.shape)
    send_left(a2l, b2l, 0)
    turn_right(b1r, 0, a2r, b2r)
    take(b1lf.at[pl.ds(0, ny - 1)], r1l.at[1])
    parts = exchange([unfold(b1lf[k].astype(F32)) for k in range(ny)], rows)
    turned = nn_dot(swap2, jnp.concatenate(parts, 0).astype(BF16))
    for k in range(nz):
        a2lf[k] = fold(turned[k * ny:(k + 1) * ny]).astype(BF16)
    send_left(a2lf, b2lf, 1)
    turn_right(b1rf, 1, a2rf, b2rf)

    for t in range(nt):
        gate[t] = jax.nn.sigmoid(nn_dot(normed[t], w_gate[...]))

    ahead = max(1, lanes // (3 * rows))
    cut = -(-ahead * rows * 3 // lanes) * (lanes // 3)
    groups = ((0, ahead), (ahead, nz))

    def forward_left(left, part, k):
        send(left.at[xl, k], left.at[xl, k], sl.at[part], rl.at[part], dev_x(xh, 1 - xl))

    def forward_right(right, dst, part, g):
        low, high = groups[g]
        for k in range(low, high):
            @pl.when(y != k)
            def _():
                take(right.at[k], r2r.at[part, k])

            send(right.at[k], dst.at[xl, k], sr.at[part, g], rr.at[part, g], dev_x(1 - xh, xh))

            @pl.when(jnp.logical_not(same))
            def _():
                send(right.at[k], dst.at[xl, k], sr.at[part, g], rr.at[part, g], dev_x(xh, xh))

        @pl.when(same)
        def _():
            dst[xl, low:high] = right[low:high]

    for part, (left, right, dst) in enumerate(((b2l, b2r, rx), (b2lf, b2rf, rxf))):
        forward_left(left, part, z)
        order = far_first(nz)[::-1]
        for place, d in enumerate(order):
            if place == len(order) // 2:
                forward_right(right, dst, part, 0)
            k = at_z(d)
            take(left.at[xl, k], r2l.at[part, k])
            forward_left(left, part, k)
    forward_right(b2r, rx, 0, 1)
    forward_right(b2rf, rxf, 1, 1)

    two = 2 * ny

    def take_right(dst, part, g, sem):
        low, high = groups[g]

        @pl.when(same)
        def _():
            take(dst.at[0, pl.ds(low, high - low)], sem.at[part, g])

        @pl.when(jnp.logical_not(same))
        def _():
            take(dst.at[:, pl.ds(low, high - low)], sem.at[part, g])

    def panel(g):
        count, keep = (ahead, cut) if g == 0 else (ny, lanes)

        def stack(parts, swap):
            return nn_dot(swap, jnp.concatenate(exchange(parts, rows, keep), 0).astype(BF16)).astype(BF16)

        return (
            lambda: jnp.concatenate([stack([rx[x, k].astype(F32) for k in range(count)], swap1) for x in range(2)], 0),
            lambda: jnp.concatenate(
                [stack([unfold(rxf[x, k].astype(F32)) for k in range(count)], swap2) for x in range(2)], 0
            ),
        )

    scale = 4.0 / math.sqrt(rows * 2 * ny)
    mine = y * nz + z
    tile_lanes = land.shape[2]

    def tile(tri, o):
        base, off = divmod(o * rows, tile_lanes)
        lane = lax.broadcasted_iota(jnp.int32, (cols, tile_lanes), 1)
        block = tri[:, base * tile_lanes:(base + 1) * tile_lanes]
        if off:
            block = pltpu.roll(block, tile_lanes - off, 1)
        if off + rows > tile_lanes:
            after = pltpu.roll(tri[:, (base + 1) * tile_lanes:(base + 2) * tile_lanes], tile_lanes - off, 1)
            block = jnp.where(lane < tile_lanes - off, block, after)
        top = jnp.where(lane[:ny] < rows, block[:ny], pltpu.roll(block[ny:two], rows, 1))
        return jnp.concatenate([top, block[two:]], 0)

    for g, (low, high) in enumerate(groups):
        if g == 0:
            take(b2l.at[0], rl.at[0])
        take_right(rx, 0, g, rr)
        panel_a, panel_b = panel(g)
        total = tn_dot(panel_a(), b2l[...].reshape(2 * nz * two, lanes))
        if g == 0:
            take(b2lf.at[0], rl.at[1])
            lefts = [unfold(b2lf[x, k].astype(F32)) for x in range(2) for k in range(nz)]
            left_b = jnp.concatenate(lefts, 0).astype(BF16)
        take_right(rxf, 1, g, rr)
        total = total + tn_dot(panel_b(), left_b)
        pp[low * rows:high * rows] = total[low * rows:high * rows]
        for k in range(low, high):
            send(pp.at[pl.ds(k * rows + (1 - core) * cols, cols)], qq.at[k], sq.at[g], rq.at[g], other_core)
        take(qq.at[pl.ds(low, high - low)], rq.at[g])
        for k in range(low, high):
            tri = (pp[pl.ds(k * rows + core * cols, cols), :] + qq[k]) * scale
            for o in range(ny):
                sc[k, o] = tile(tri, o).astype(BF16)
            for d in far_first(ny):
                to = at_y(d)
                send(sc.at[k, to], land.at[mine], s3, r3, (to * 2 + xh, k * 4 + xl * 2 + core))

            @pl.when(z != k)
            def _():
                send(sc.at[k, y], land.at[mine], s3, r3, dev_z(k))
    land[mine] = sc[z, y]

    take(land.at[pl.ds(0, chans - 1)], r3)
    f32[...] = land[...].astype(F32).reshape(f32.shape)
    picked = [f32[pl.ds(r, chans, stride=two), :] for r in range(two)]
    side = lax.broadcasted_iota(jnp.int32, picked[0].shape, 1) < rows
    for r in range(ny, two, 2):
        picked[r] = jnp.where(side, picked[r], pltpu.roll(picked[r + 1], rows, 1))
    places = [(r, r + ny) for r in range(ny)] + [(r, r + 1) for r in range(two, cols, 2)]
    mixed = tn_dot(jnp.concatenate(picked[:ny] + picked[ny::2], 1).astype(BF16), w_out[...])
    for index, pair_of in enumerate(places):
        for half, j in enumerate(pair_of):
            start = index * tile_lanes + half * rows
            t, at = j // ny, j % ny * rows
            out[j] = (gate[t, at:at + rows, :] * mixed[start:start + rows]).astype(BF16)

    for part, (first, second, third) in enumerate(((a1l, a2l, rx), (a1lf, a2lf, rxf))):
        take(first.at[pl.ds(0, ny - 1)], s1l.at[part])
        take(first.at[pl.ds(0, nz - 1)], s1r.at[part])
        take(second.at[pl.ds(0, nz - 1)], s2l.at[part])
        take(second.at[pl.ds(0, ny - 1)], s2r.at[part])
        take(third.at[0], sl.at[part])

        for g in range(2):
            take_right(third, part, g, sr)
    for g, (low, high) in enumerate(groups):
        take(qq.at[pl.ds(low, high - low)], sq.at[g])
    take(land.at[pl.ds(0, chans - 1)], s3)


def per_device(ny, nz, pair, token_mask, ln_gain, ln_bias, w_left, w_right, w_gate, w_out):
    rows, cols, width = pair.shape
    lanes = ny * rows
    nt = cols // ny
    chans = ny * nz
    third = 2 * lanes // 3
    dma = pltpu.SemaphoreType.DMA
    swapped = pl.pallas_call(
        functools.partial(kernel, ny, nz),
        out_shape=pltpu.VMEM((cols, rows, width), BF16),
        in_specs=[pl.BlockSpec(memory_space=pl.ANY)] * 8,
        out_specs=pl.BlockSpec(memory_space=pltpu.VMEM),
        scratch_shapes=[
            pltpu.SMEM(token_mask.shape, jnp.int32),
            pltpu.VMEM(pair.shape, BF16),
            pltpu.VMEM((1, width), F32),
            pltpu.VMEM((1, width), F32),
            pltpu.VMEM(w_left.shape, BF16),
            pltpu.VMEM(w_right.shape, BF16),
            pltpu.VMEM(w_gate.shape, BF16),
            pltpu.VMEM(w_out.shape, BF16),
            dma((8,)),
            pltpu.VMEM((nt, rows * ny, width), F32),
            pltpu.VMEM((nt, rows * ny, width), BF16),
            pltpu.VMEM((nt, rows * ny, width), F32),
            pltpu.VMEM((4 * chans, width), BF16),
            pltpu.VMEM((ny, 2 * nz, lanes), BF16),
            pltpu.VMEM((ny, 2 * nz, third), BF16),
            pltpu.VMEM((ny, 2 * nz, lanes), BF16),
            pltpu.VMEM((ny, 2 * nz, third), BF16),
            pltpu.VMEM((nz, 2 * ny, lanes), BF16),
            pltpu.VMEM((nz, 2 * ny, third), BF16),
            pltpu.VMEM((nz, 2 * ny, lanes), BF16),
            pltpu.VMEM((nz, 2 * ny, third), BF16),
            pltpu.VMEM((nz, 2 * ny, lanes), BF16),
            pltpu.VMEM((nz, 2 * ny, third), BF16),
            pltpu.VMEM((2, nz, 2 * ny, lanes), BF16),
            pltpu.VMEM((2, nz, 2 * ny, third), BF16),
            pltpu.VMEM((ny, 2 * nz, lanes), BF16),
            pltpu.VMEM((ny, 2 * nz, third), BF16),
            pltpu.VMEM((ny, 2 * nz, lanes), BF16),
            pltpu.VMEM((ny, 2 * nz, third), BF16),
            pltpu.VMEM((2, ny, 2 * nz, lanes), BF16),
            pltpu.VMEM((2, ny, 2 * nz, third), BF16),
            pltpu.VMEM((lanes, lanes), F32),
            pltpu.VMEM((nz, cols, lanes), F32),
            pltpu.VMEM((nz, ny, 2 * ny, min(lanes, 128)), BF16),
            pltpu.VMEM((chans, 2 * ny, min(lanes, 128)), BF16),
            pltpu.VMEM((chans * 2 * ny, min(lanes, 128)), F32),
        ] + [dma((2,))] * 4 + [dma((2,)), dma((2, nz)), dma((2,)), dma((2, ny))] + [dma((2,))] * 2 + [dma((2, 2))] * 2 + [dma((2,))] * 2 + [dma] * 2,
        compiler_params=pltpu.CompilerParams(
            collective_id=0, has_side_effects=True, vmem_limit_bytes=60 * 1024 * 1024
        ),
    )(token_mask, pair, ln_gain.reshape(1, width), ln_bias.reshape(1, width), w_left, w_right, w_gate, w_out)
    return jnp.transpose(swapped, (1, 0, 2))


def solution(mesh):
    ny, nz = mesh.shape["row"] // 2, mesh.shape["col"] // 4
    placed = (P("row", "col", None), P(), P(), P(), P(), P(), P(), P())
    return jax.shard_map(
        functools.partial(per_device, ny, nz), mesh=mesh, in_specs=placed,
        out_specs=P("row", "col", None), check_vma=False,
    )
```

```python
import functools
import math

import jax
import jax.numpy as jnp
from jax import lax
from jax.experimental import pallas as pl
from jax.experimental.pallas import tpu as pltpu
from jax.sharding import PartitionSpec as P

F32 = jnp.float32
BF16 = jnp.bfloat16
MESH = pl.DeviceIdType.MESH


def one_hot(shape, source):
    row = lax.broadcasted_iota(jnp.int32, shape, 0)
    col = lax.broadcasted_iota(jnp.int32, shape, 1)
    return row, col, source(row)


def permutation(count, source):
    _, col, src = one_hot((count, count), source)
    return jnp.where(col == src, 1.0, 0.0).astype(BF16)


def swap_ends(a, b, c):
    return permutation(a * b * c, lambda o: (o % a) * (b * c) + ((o // a) % b) * c + o // (a * b))


def far_first(n):
    return sorted(range(1, n), key=lambda d: -min(d, n - d))


def nt_dot(x, y):
    return lax.dot_general(x, y, (((1,), (1,)), ((), ())), preferred_element_type=F32)


def tn_dot(x, y):
    return lax.dot_general(x, y, (((0,), (0,)), ((), ())), preferred_element_type=F32)


def nn_dot(x, y):
    return lax.dot_general(x, y, (((1,), (0,)), ((), ())), preferred_element_type=F32)


def spread(parts, width):
    return [pltpu.roll(part, y * width, 1) if y else part for y, part in enumerate(parts)]


def pick(rolled, width, k, keep=None):
    total = rolled[0].shape[1]
    n = total // width
    pos = lax.broadcasted_iota(jnp.int32, rolled[0].shape, 1) // width
    picked = rolled[0]
    for y, part in list(enumerate(rolled))[1:]:
        picked = jnp.where(pos == (k + y) % n, part, picked)
    return (pltpu.roll(picked, total - k * width, 1) if k else picked)[:, :keep]


def exchange(parts, width, keep=None):
    rolled = spread(parts, width)
    return [pick(rolled, width, k, keep) for k in range(parts[0].shape[1] // width)]


def fold(block):
    third = block.shape[1] // 3
    a, b, c = (block[:, i * third:(i + 1) * third] for i in range(3))
    return jnp.concatenate(
        [jnp.concatenate([a, b], 0), jnp.concatenate([c, jnp.zeros_like(c)], 0)], 1
    )


def unfold(block):
    n, third = block.shape[0] // 2, block.shape[1] // 2
    return jnp.concatenate([block[:n, :third], block[n:, :third], block[:n, third:]], 1)


def kernel(
    ny, nz, tm_hbm, pair_hbm, gain_hbm, bias_hbm, wl_hbm, wr_hbm, wg_hbm, wo_hbm, out,
    tm, pair, gain, bias, w_left, w_right, w_gate, w_out, load, n32, normed, gate, wt,
    a1l, a1lf, b1l, b1lf, a1r, a1rf, b1r, b1rf, a2l, a2lf, b2l, b2lf, a2r, a2rf, b2r, b2rf, rx, rxf,
    pp, qq, sc, land, f32,
    s1l, r1l, s1r, r1r, s2l, r2l, s2r, r2r, sl, rl, sr, rr, sq, rq, s3, r3,
):
    cols, rows, width = out.shape
    nt = cols // ny
    lanes = ny * rows
    chans = ny * nz
    loads = [
        pltpu.make_async_copy(src, dst, load.at[i])
        for i, (src, dst) in enumerate((
            (pair_hbm, pair), (wl_hbm, w_left), (wr_hbm, w_right), (tm_hbm, tm),
            (gain_hbm, gain), (bias_hbm, bias), (wg_hbm, w_gate), (wo_hbm, w_out),
        ))
    ]
    row, col = lax.axis_index("row"), lax.axis_index("col")
    y, xh = row // 2, row % 2
    z, xl, core = col // 4, (col // 2) % 2, col % 2
    same = xl == xh

    def at_y(d):
        return lax.rem(y + d, ny)

    def at_z(d):
        return lax.rem(z + d, nz)

    def dev_y(other):
        return (other * 2 + xh, col)

    def dev_z(other):
        return (row, other * 4 + xl * 2 + core)

    def dev_x(oh, ol):
        return (y * 2 + oh, z * 4 + ol * 2 + core)

    other_core = (row, z * 4 + xl * 2 + 1 - core)
    peers = [dev_y(at_y(d)) for d in far_first(ny)] + [dev_z(at_z(d)) for d in far_first(nz)]
    peers += [dev_x(xh, 1 - xl), dev_x(1 - xh, xl), dev_x(1 - xh, 1 - xl), other_core]
    barrier = pltpu.get_barrier_semaphore()
    for peer in peers:
        pl.semaphore_signal(barrier, inc=1, device_id=peer, device_id_type=MESH)

    for copy in loads:
        copy.start()

    def send(src, dst, send_sem, recv_sem, device):
        pltpu.make_async_remote_copy(
            src_ref=src, dst_ref=dst, send_sem=send_sem, recv_sem=recv_sem,
            device_id=device, device_id_type=MESH,
        ).start()

    def take(ref, sem):
        pltpu.make_async_copy(ref, ref, sem).wait()

    for copy in loads[1:]:
        copy.wait()

    _, c, r = one_hot((2 * chans, 2 * chans), lambda o: o)
    wt[0:2 * chans, :] = nt_dot(jnp.where(c == r, 1.0, 0.0).astype(BF16), w_left[...]).astype(BF16)
    _, c, r = one_hot(
        (2 * chans, 2 * chans), lambda o: (o // chans) * chans + (o % ny) * nz + (o % chans) // ny
    )
    wt[2 * chans:4 * chans, :] = nt_dot(jnp.where(c == r, 1.0, 0.0).astype(BF16), w_right[...]).astype(BF16)

    lane = lax.broadcasted_iota(jnp.int32, (1, lanes), 1)
    row_mask = jnp.zeros((1, lanes), F32)
    for i in range(rows):
        row_mask = jnp.where(lane % rows == i, tm[row * rows + i].astype(F32), row_mask)

    def mask_of(t):
        col_mask = jnp.zeros((1, lanes), F32)
        for k in range(ny):
            col_mask = jnp.where(lane // rows == k, tm[col * cols + t * ny + k].astype(F32), col_mask)
        return row_mask * col_mask

    def project(t):
        block = pair[...].astype(F32).reshape(rows, cols, width)[:, t * ny:(t + 1) * ny, :]
        center = jnp.mean(block, axis=-1, keepdims=True)
        delta = block - center
        spread = jnp.mean(delta * delta, axis=-1, keepdims=True)
        value = delta * lax.rsqrt(spread + 1e-05) * gain[...].reshape(1, 1, width) + bias[...].reshape(1, 1, width)
        n32[t] = value.reshape(rows * ny, width)
        for k in range(ny):
            normed[t, k * rows:(k + 1) * rows, :] = n32[t, pl.ds(k, rows, stride=ny), :].astype(BF16)
        proj = nt_dot(wt[...], normed[t])
        mask = mask_of(t)
        sides = (proj[:2 * chans], proj[2 * chans:])
        return [jax.nn.sigmoid(side[:chans]) * side[chans:] * mask for side in sides]

    swap1 = swap_ends(ny, 2, nz)
    swap2 = swap_ends(ny, 1, nz)

    def send_first(left, left_land, right, right_land, part):
        for d in far_first(ny):
            to = at_y(d)
            send(left.at[to], left_land.at[y], s1l.at[part], r1l.at[part], dev_y(to))
        for d in far_first(nz):
            to = at_z(d)
            send(right.at[to], right_land.at[z], s1r.at[part], r1r.at[part], dev_z(to))
        left_land[y] = left[y]
        right_land[z] = right[z]

    loads[0].wait()
    left0, right0 = project(0)
    left1, right1 = project(1)
    pairs = lambda u, v, n: jnp.concatenate([u.reshape(n, -1, lanes), v.reshape(n, -1, lanes)], 1).astype(BF16)
    a1l[...] = pairs(left0, left1, ny)
    a1r[...] = pairs(right0, right1, nz)
    pl.semaphore_wait(barrier, len(peers))
    send_first(a1l, b1l, a1r, b1r, 0)
    left2, right2 = project(2)
    for k in range(ny):
        a1lf[k] = fold(left2[k * nz:(k + 1) * nz]).astype(BF16)
    for k in range(nz):
        a1rf[k] = fold(right2[k * ny:(k + 1) * ny]).astype(BF16)
    send_first(a1lf, b1lf, a1rf, b1rf, 1)

    def turn_right(land, part, out_buf, dst):
        take(land.at[pl.ds(0, nz - 1)], r1r.at[part])
        out_buf[...] = nn_dot(swap1, land[...].reshape(nz * 2 * ny, -1)).astype(BF16).reshape(out_buf.shape)
        for d in far_first(ny):
            to = at_y(d)
            send(out_buf.at[to], dst.at[y], s2r.at[part], r2r.at[part, y], dev_y(to))
        dst[y] = out_buf[y]

    def send_left(out_buf, dst, part):
        for d in far_first(nz):
            to = at_z(d)
            send(out_buf.at[to], dst.at[xl, z], s2l.at[part], r2l.at[part, z], dev_z(to))
        dst[xl, z] = out_buf[z]

    take(b1l.at[pl.ds(0, ny - 1)], r1l.at[0])
    parts = exchange([b1l[k].astype(F32) for k in range(ny)], rows)
    a2l[...] = nn_dot(swap1, jnp.concatenate(parts, 0).astype(BF16)).astype(BF16).reshape(a2l.shape)
    send_left(a2l, b2l, 0)
    turn_right(b1r, 0, a2r, b2r)
    take(b1lf.at[pl.ds(0, ny - 1)], r1l.at[1])
    parts = exchange([unfold(b1lf[k].astype(F32)) for k in range(ny)], rows)
    turned = nn_dot(swap2, jnp.concatenate(parts, 0).astype(BF16))
    for k in range(nz):
        a2lf[k] = fold(turned[k * ny:(k + 1) * ny]).astype(BF16)
    send_left(a2lf, b2lf, 1)
    turn_right(b1rf, 1, a2rf, b2rf)

    for t in range(nt):
        gate[t] = jax.nn.sigmoid(nn_dot(normed[t], w_gate[...]))

    ahead = max(1, lanes // (3 * rows))
    cut = -(-ahead * rows * 3 // lanes) * (lanes // 3)
    groups = ((0, ahead), (ahead, nz))

    def forward_left(left, part, k):
        send(left.at[xl, k], left.at[xl, k], sl.at[part], rl.at[part], dev_x(xh, 1 - xl))

    def forward_right(right, dst, part, g):
        low, high = groups[g]
        for k in range(low, high):
            @pl.when(y != k)
            def _():
                take(right.at[k], r2r.at[part, k])

            send(right.at[k], dst.at[xl, k], sr.at[part, g], rr.at[part, g], dev_x(1 - xh, xh))

            @pl.when(jnp.logical_not(same))
            def _():
                send(right.at[k], dst.at[xl, k], sr.at[part, g], rr.at[part, g], dev_x(xh, xh))

        @pl.when(same)
        def _():
            dst[xl, low:high] = right[low:high]

    for part, (left, right, dst) in enumerate(((b2l, b2r, rx), (b2lf, b2rf, rxf))):
        forward_left(left, part, z)
        order = far_first(nz)[::-1]
        for place, d in enumerate(order):
            if place == len(order) // 2:
                forward_right(right, dst, part, 0)
            k = at_z(d)
            take(left.at[xl, k], r2l.at[part, k])
            forward_left(left, part, k)
    forward_right(b2r, rx, 0, 1)
    forward_right(b2rf, rxf, 1, 1)

    two = 2 * ny

    def take_right(dst, part, g, sem):
        low, high = groups[g]

        @pl.when(same)
        def _():
            take(dst.at[0, pl.ds(low, high - low)], sem.at[part, g])

        @pl.when(jnp.logical_not(same))
        def _():
            take(dst.at[:, pl.ds(low, high - low)], sem.at[part, g])

    def panel(g):
        count, keep = (ahead, cut) if g == 0 else (ny, lanes)

        def stack(parts):
            return jnp.concatenate(exchange(parts, rows, keep), 0).astype(BF16)

        return (
            lambda: jnp.concatenate([stack([rx[x, k].astype(F32) for k in range(count)]) for x in range(2)], 0),
            lambda: jnp.concatenate(
                [stack([unfold(rxf[x, k].astype(F32)) for k in range(count)]) for x in range(2)], 0
            ),
        )

    scale = 4.0 / math.sqrt(rows * 2 * ny)
    mine = y * nz + z
    tile_lanes = land.shape[2]

    def tile(tri, o):
        base, off = divmod(o * rows, tile_lanes)
        lane = lax.broadcasted_iota(jnp.int32, (cols, tile_lanes), 1)
        block = tri[:, base * tile_lanes:(base + 1) * tile_lanes]
        if off:
            block = pltpu.roll(block, tile_lanes - off, 1)
        if off + rows > tile_lanes:
            after = pltpu.roll(tri[:, (base + 1) * tile_lanes:(base + 2) * tile_lanes], tile_lanes - off, 1)
            block = jnp.where(lane < tile_lanes - off, block, after)
        top = jnp.where(lane[:ny] < rows, block[:ny], pltpu.roll(block[ny:two], rows, 1))
        return jnp.concatenate([top, block[two:]], 0)

    for g, (low, high) in enumerate(groups):
        if g == 0:
            take(b2l.at[0], rl.at[0])
            left_a = [nn_dot(swap1, b2l[x].reshape(nz * two, lanes)).astype(BF16) for x in range(2)]
            left_a = jnp.concatenate(left_a, 0)
        take_right(rx, 0, g, rr)
        panel_a, panel_b = panel(g)
        total = tn_dot(panel_a(), left_a)
        if g == 0:
            take(b2lf.at[0], rl.at[1])
            lefts = [jnp.concatenate([unfold(b2lf[x, k].astype(F32)) for k in range(nz)], 0) for x in range(2)]
            left_b = jnp.concatenate([nn_dot(swap2, left.astype(BF16)).astype(BF16) for left in lefts], 0)
        take_right(rxf, 1, g, rr)
        total = total + tn_dot(panel_b(), left_b)
        pp[low * rows:high * rows] = total[low * rows:high * rows]
        for k in range(low, high):
            send(pp.at[pl.ds(k * rows + (1 - core) * cols, cols)], qq.at[k], sq.at[g], rq.at[g], other_core)
        take(qq.at[pl.ds(low, high - low)], rq.at[g])
        for k in range(low, high):
            tri = (pp[pl.ds(k * rows + core * cols, cols), :] + qq[k]) * scale
            for o in range(ny):
                sc[k, o] = tile(tri, o).astype(BF16)
            for d in far_first(ny)[::-1]:
                to = at_y(d)
                send(sc.at[k, to], land.at[mine], s3, r3, (to * 2 + xh, k * 4 + xl * 2 + core))

            @pl.when(z != k)
            def _():
                send(sc.at[k, y], land.at[mine], s3, r3, dev_z(k))
    land[mine] = sc[z, y]

    for part, (first, second, third) in enumerate(((a1l, a2l, rx), (a1lf, a2lf, rxf))):
        take(first.at[pl.ds(0, ny - 1)], s1l.at[part])
        take(first.at[pl.ds(0, nz - 1)], s1r.at[part])
        take(second.at[pl.ds(0, nz - 1)], s2l.at[part])
        take(second.at[pl.ds(0, ny - 1)], s2r.at[part])
        take(third.at[0], sl.at[part])

        for g in range(2):
            take_right(third, part, g, sr)
    for g, (low, high) in enumerate(groups):
        take(qq.at[pl.ds(low, high - low)], sq.at[g])

    take(land.at[pl.ds(0, chans - 1)], r3)
    f32[...] = land[...].astype(F32).reshape(f32.shape)
    picked = [f32[pl.ds(r, chans, stride=two), :] for r in range(two)]
    side = lax.broadcasted_iota(jnp.int32, picked[0].shape, 1) < rows
    for r in range(ny, two, 2):
        picked[r] = jnp.where(side, picked[r], pltpu.roll(picked[r + 1], rows, 1))
    places = [(r, r + ny) for r in range(ny)] + [(r, r + 1) for r in range(two, cols, 2)]
    mixed = tn_dot(jnp.concatenate(picked[:ny] + picked[ny::2], 1).astype(BF16), w_out[...])
    for index, pair_of in enumerate(places):
        for half, j in enumerate(pair_of):
            start = index * tile_lanes + half * rows
            t, at = j // ny, j % ny * rows
            out[j] = (gate[t, at:at + rows, :] * mixed[start:start + rows]).astype(BF16)

    take(land.at[pl.ds(0, chans - 1)], s3)


def per_device(ny, nz, pair, token_mask, ln_gain, ln_bias, w_left, w_right, w_gate, w_out):
    rows, cols, width = pair.shape
    lanes = ny * rows
    nt = cols // ny
    chans = ny * nz
    third = 2 * lanes // 3
    dma = pltpu.SemaphoreType.DMA
    swapped = pl.pallas_call(
        functools.partial(kernel, ny, nz),
        out_shape=pltpu.VMEM((cols, rows, width), BF16),
        in_specs=[pl.BlockSpec(memory_space=pl.ANY)] * 8,
        out_specs=pl.BlockSpec(memory_space=pltpu.VMEM),
        scratch_shapes=[
            pltpu.SMEM(token_mask.shape, jnp.int32),
            pltpu.VMEM((rows * cols, width), BF16),
            pltpu.VMEM((1, width), F32),
            pltpu.VMEM((1, width), F32),
            pltpu.VMEM(w_left.shape, BF16),
            pltpu.VMEM(w_right.shape, BF16),
            pltpu.VMEM(w_gate.shape, BF16),
            pltpu.VMEM(w_out.shape, BF16),
            dma((8,)),
            pltpu.VMEM((nt, rows * ny, width), F32),
            pltpu.VMEM((nt, rows * ny, width), BF16),
            pltpu.VMEM((nt, rows * ny, width), F32),
            pltpu.VMEM((4 * chans, width), BF16),
            pltpu.VMEM((ny, 2 * nz, lanes), BF16),
            pltpu.VMEM((ny, 2 * nz, third), BF16),
            pltpu.VMEM((ny, 2 * nz, lanes), BF16),
            pltpu.VMEM((ny, 2 * nz, third), BF16),
            pltpu.VMEM((nz, 2 * ny, lanes), BF16),
            pltpu.VMEM((nz, 2 * ny, third), BF16),
            pltpu.VMEM((nz, 2 * ny, lanes), BF16),
            pltpu.VMEM((nz, 2 * ny, third), BF16),
            pltpu.VMEM((nz, 2 * ny, lanes), BF16),
            pltpu.VMEM((nz, 2 * ny, third), BF16),
            pltpu.VMEM((2, nz, 2 * ny, lanes), BF16),
            pltpu.VMEM((2, nz, 2 * ny, third), BF16),
            pltpu.VMEM((ny, 2 * nz, lanes), BF16),
            pltpu.VMEM((ny, 2 * nz, third), BF16),
            pltpu.VMEM((ny, 2 * nz, lanes), BF16),
            pltpu.VMEM((ny, 2 * nz, third), BF16),
            pltpu.VMEM((2, ny, 2 * nz, lanes), BF16),
            pltpu.VMEM((2, ny, 2 * nz, third), BF16),
            pltpu.VMEM((lanes, lanes), F32),
            pltpu.VMEM((nz, cols, lanes), F32),
            pltpu.VMEM((nz, ny, 2 * ny, min(lanes, 128)), BF16),
            pltpu.VMEM((chans, 2 * ny, min(lanes, 128)), BF16),
            pltpu.VMEM((chans * 2 * ny, min(lanes, 128)), F32),
        ] + [dma((2,))] * 4 + [dma((2,)), dma((2, nz)), dma((2,)), dma((2, ny))] + [dma((2,))] * 2 + [dma((2, 2))] * 2 + [dma((2,))] * 2 + [dma] * 2,
        compiler_params=pltpu.CompilerParams(
            collective_id=0, has_side_effects=True, vmem_limit_bytes=60 * 1024 * 1024
        ),
    )(token_mask, pair.reshape(rows * cols, width), ln_gain.reshape(1, width), ln_bias.reshape(1, width), w_left, w_right, w_gate, w_out)
    return jnp.transpose(swapped, (1, 0, 2))


def solution(mesh):
    ny, nz = mesh.shape["row"] // 2, mesh.shape["col"] // 4
    placed = (P("row", "col", None), P(), P(), P(), P(), P(), P(), P())
    return jax.shard_map(
        functools.partial(per_device, ny, nz), mesh=mesh, in_specs=placed,
        out_specs=P("row", "col", None), check_vma=False,
    )
```

```python
import functools
import math

import jax
import jax.numpy as jnp
from jax import lax
from jax.experimental import pallas as pl
from jax.experimental.pallas import tpu as pltpu
from jax.sharding import PartitionSpec as P

F32 = jnp.float32
BF16 = jnp.bfloat16
MESH = pl.DeviceIdType.MESH


def one_hot(shape, source):
    row = lax.broadcasted_iota(jnp.int32, shape, 0)
    col = lax.broadcasted_iota(jnp.int32, shape, 1)
    return row, col, source(row)


def permutation(count, source):
    _, col, src = one_hot((count, count), source)
    return jnp.where(col == src, 1.0, 0.0).astype(BF16)


def swap_ends(a, b, c):
    return permutation(a * b * c, lambda o: (o % a) * (b * c) + ((o // a) % b) * c + o // (a * b))


def far_first(n):
    return sorted(range(1, n), key=lambda d: -min(d, n - d))


def nt_dot(x, y):
    return lax.dot_general(x, y, (((1,), (1,)), ((), ())), preferred_element_type=F32)


def tn_dot(x, y):
    return lax.dot_general(x, y, (((0,), (0,)), ((), ())), preferred_element_type=F32)


def nn_dot(x, y):
    return lax.dot_general(x, y, (((1,), (0,)), ((), ())), preferred_element_type=F32)


def spread(parts, width):
    return [pltpu.roll(part, y * width, 1) if y else part for y, part in enumerate(parts)]


def pick(rolled, width, k, keep=None):
    total = rolled[0].shape[1]
    n = total // width
    pos = lax.broadcasted_iota(jnp.int32, rolled[0].shape, 1) // width
    picked = rolled[0]
    for y, part in list(enumerate(rolled))[1:]:
        picked = jnp.where(pos == (k + y) % n, part, picked)
    return (pltpu.roll(picked, total - k * width, 1) if k else picked)[:, :keep]


def exchange(parts, width, keep=None):
    rolled = spread(parts, width)
    return [pick(rolled, width, k, keep) for k in range(parts[0].shape[1] // width)]


def fold(block):
    third = block.shape[1] // 3
    a, b, c = (block[:, i * third:(i + 1) * third] for i in range(3))
    return jnp.concatenate(
        [jnp.concatenate([a, b], 0), jnp.concatenate([c, jnp.zeros_like(c)], 0)], 1
    )


def unfold(block):
    n, third = block.shape[0] // 2, block.shape[1] // 2
    return jnp.concatenate([block[:n, :third], block[n:, :third], block[:n, third:]], 1)


def kernel(
    ny, nz, tm_hbm, pair_hbm, gain_hbm, bias_hbm, wl_hbm, wr_hbm, wg_hbm, wo_hbm, out,
    tm, pair, gain, bias, w_left, w_right, w_gate, w_out, load, n32, normed, gate, wt,
    a1l, a1lf, b1l, b1lf, a1r, a1rf, b1r, b1rf, a2l, a2lf, b2l, b2lf, a2r, a2rf, b2r, b2rf, rx, rxf,
    pp, qq, sc, land, f32,
    s1l, r1l, s1r, r1r, s2l, r2l, s2r, r2r, sl, rl, sr, rr, sq, rq, s3, r3,
):
    cols, rows, width = out.shape
    nt = cols // ny
    lanes = ny * rows
    chans = ny * nz
    loads = [
        pltpu.make_async_copy(src, dst, load.at[i])
        for i, (src, dst) in enumerate((
            (pair_hbm, pair), (wl_hbm, w_left), (wr_hbm, w_right), (tm_hbm, tm),
            (gain_hbm, gain), (bias_hbm, bias), (wg_hbm, w_gate), (wo_hbm, w_out),
        ))
    ]
    row, col = lax.axis_index("row"), lax.axis_index("col")
    y, xh = row // 2, row % 2
    z, xl, core = col // 4, (col // 2) % 2, col % 2
    same = xl == xh

    def at_y(d):
        return lax.rem(y + d, ny)

    def at_z(d):
        return lax.rem(z + d, nz)

    def dev_y(other):
        return (other * 2 + xh, col)

    def dev_z(other):
        return (row, other * 4 + xl * 2 + core)

    def dev_x(oh, ol):
        return (y * 2 + oh, z * 4 + ol * 2 + core)

    other_core = (row, z * 4 + xl * 2 + 1 - core)
    peers = [dev_y(at_y(d)) for d in far_first(ny)] + [dev_z(at_z(d)) for d in far_first(nz)]
    peers += [dev_x(xh, 1 - xl), dev_x(1 - xh, xl), dev_x(1 - xh, 1 - xl), other_core]
    barrier = pltpu.get_barrier_semaphore()
    for peer in peers:
        pl.semaphore_signal(barrier, inc=1, device_id=peer, device_id_type=MESH)

    for copy in loads:
        copy.start()

    def send(src, dst, send_sem, recv_sem, device):
        pltpu.make_async_remote_copy(
            src_ref=src, dst_ref=dst, send_sem=send_sem, recv_sem=recv_sem,
            device_id=device, device_id_type=MESH,
        ).start()

    def take(ref, sem):
        pltpu.make_async_copy(ref, ref, sem).wait()

    for copy in loads[1:]:
        copy.wait()

    _, c, r = one_hot((2 * chans, 2 * chans), lambda o: o)
    wt[0:2 * chans, :] = nt_dot(jnp.where(c == r, 1.0, 0.0).astype(BF16), w_left[...]).astype(BF16)
    _, c, r = one_hot(
        (2 * chans, 2 * chans), lambda o: (o // chans) * chans + (o % ny) * nz + (o % chans) // ny
    )
    wt[2 * chans:4 * chans, :] = nt_dot(jnp.where(c == r, 1.0, 0.0).astype(BF16), w_right[...]).astype(BF16)

    lane = lax.broadcasted_iota(jnp.int32, (1, lanes), 1)
    row_mask = jnp.zeros((1, lanes), F32)
    for i in range(rows):
        row_mask = jnp.where(lane % rows == i, tm[row * rows + i].astype(F32), row_mask)

    def mask_of(t):
        col_mask = jnp.zeros((1, lanes), F32)
        for k in range(ny):
            col_mask = jnp.where(lane // rows == k, tm[col * cols + t * ny + k].astype(F32), col_mask)
        return row_mask * col_mask

    def project(t):
        block = pair[...].astype(F32).reshape(rows, cols, width)[:, t * ny:(t + 1) * ny, :]
        center = jnp.mean(block, axis=-1, keepdims=True)
        delta = block - center
        spread = jnp.mean(delta * delta, axis=-1, keepdims=True)
        value = delta * lax.rsqrt(spread + 1e-05) * gain[...].reshape(1, 1, width) + bias[...].reshape(1, 1, width)
        n32[t] = value.reshape(rows * ny, width)
        for k in range(ny):
            normed[t, k * rows:(k + 1) * rows, :] = n32[t, pl.ds(k, rows, stride=ny), :].astype(BF16)
        proj = nt_dot(wt[...], normed[t])
        mask = mask_of(t)
        sides = (proj[:2 * chans], proj[2 * chans:])
        return [jax.nn.sigmoid(side[:chans]) * side[chans:] * mask for side in sides]

    swap1 = swap_ends(ny, 2, nz)
    swap2 = swap_ends(ny, 1, nz)

    def send_first(left, left_land, right, right_land, part):
        for d in far_first(ny):
            to = at_y(d)
            send(left.at[to], left_land.at[y], s1l.at[part], r1l.at[part], dev_y(to))
            to = at_z(d)
            send(right.at[to], right_land.at[z], s1r.at[part], r1r.at[part], dev_z(to))
        left_land[y] = left[y]
        right_land[z] = right[z]

    loads[0].wait()
    left0, right0 = project(0)
    left1, right1 = project(1)
    pairs = lambda u, v, n: jnp.concatenate([u.reshape(n, -1, lanes), v.reshape(n, -1, lanes)], 1).astype(BF16)
    a1l[...] = pairs(left0, left1, ny)
    a1r[...] = pairs(right0, right1, nz)
    pl.semaphore_wait(barrier, len(peers))
    send_first(a1l, b1l, a1r, b1r, 0)
    left2, right2 = project(2)
    for k in range(ny):
        a1lf[k] = fold(left2[k * nz:(k + 1) * nz]).astype(BF16)
    for k in range(nz):
        a1rf[k] = fold(right2[k * ny:(k + 1) * ny]).astype(BF16)
    send_first(a1lf, b1lf, a1rf, b1rf, 1)

    def turn_right(land, part, out_buf, dst):
        take(land.at[pl.ds(0, nz - 1)], r1r.at[part])
        out_buf[...] = nn_dot(swap1, land[...].reshape(nz * 2 * ny, -1)).astype(BF16).reshape(out_buf.shape)
        for d in far_first(ny):
            to = at_y(d)
            send(out_buf.at[to], dst.at[y], s2r.at[part], r2r.at[part, y], dev_y(to))
        dst[y] = out_buf[y]

    def send_left(out_buf, dst, part):
        for d in far_first(nz):
            to = at_z(d)
            send(out_buf.at[to], dst.at[xl, z], s2l.at[part], r2l.at[part, z], dev_z(to))
        dst[xl, z] = out_buf[z]

    take(b1l.at[pl.ds(0, ny - 1)], r1l.at[0])
    parts = exchange([b1l[k].astype(F32) for k in range(ny)], rows)
    a2l[...] = nn_dot(swap1, jnp.concatenate(parts, 0).astype(BF16)).astype(BF16).reshape(a2l.shape)
    send_left(a2l, b2l, 0)
    turn_right(b1r, 0, a2r, b2r)
    take(b1lf.at[pl.ds(0, ny - 1)], r1l.at[1])
    parts = exchange([unfold(b1lf[k].astype(F32)) for k in range(ny)], rows)
    turned = nn_dot(swap2, jnp.concatenate(parts, 0).astype(BF16))
    for k in range(nz):
        a2lf[k] = fold(turned[k * ny:(k + 1) * ny]).astype(BF16)
    send_left(a2lf, b2lf, 1)
    def forward_left(left, part, k):
        send(left.at[xl, k], left.at[xl, k], sl.at[part], rl.at[part], dev_x(xh, 1 - xl))

    forward_left(b2l, 0, z)
    turn_right(b1rf, 1, a2rf, b2rf)

    ahead = max(1, lanes // (3 * rows))
    cut = -(-ahead * rows * 3 // lanes) * (lanes // 3)
    groups = ((0, ahead), (ahead, nz))

    def forward_right(right, dst, part, g):
        low, high = groups[g]
        for k in range(low, high):
            @pl.when(y != k)
            def _():
                take(right.at[k], r2r.at[part, k])

            send(right.at[k], dst.at[xl, k], sr.at[part, g], rr.at[part, g], dev_x(1 - xh, xh))

            @pl.when(jnp.logical_not(same))
            def _():
                send(right.at[k], dst.at[xl, k], sr.at[part, g], rr.at[part, g], dev_x(xh, xh))

        @pl.when(same)
        def _():
            dst[xl, low:high] = right[low:high]

    for part, (left, right, dst) in enumerate(((b2l, b2r, rx), (b2lf, b2rf, rxf))):
        if part:
            forward_left(left, part, z)
        order = far_first(nz)[::-1]
        for place, d in enumerate(order):
            if place == len(order) // 2:
                forward_right(right, dst, part, 0)
            k = at_z(d)
            take(left.at[xl, k], r2l.at[part, k])
            forward_left(left, part, k)
    forward_right(b2r, rx, 0, 1)
    forward_right(b2rf, rxf, 1, 1)

    two = 2 * ny

    def take_right(dst, part, g, sem):
        low, high = groups[g]

        @pl.when(same)
        def _():
            take(dst.at[0, pl.ds(low, high - low)], sem.at[part, g])

        @pl.when(jnp.logical_not(same))
        def _():
            take(dst.at[:, pl.ds(low, high - low)], sem.at[part, g])

    def panel(g):
        count, keep = (ahead, cut) if g == 0 else (ny, lanes)

        def stack(parts):
            return jnp.concatenate(exchange(parts, rows, keep), 0).astype(BF16)

        return (
            lambda: jnp.concatenate([stack([rx[x, k].astype(F32) for k in range(count)]) for x in range(2)], 0),
            lambda: jnp.concatenate(
                [stack([unfold(rxf[x, k].astype(F32)) for k in range(count)]) for x in range(2)], 0
            ),
        )

    scale = 4.0 / math.sqrt(rows * 2 * ny)
    mine = y * nz + z
    tile_lanes = land.shape[2]

    def tile(tri, o):
        base, off = divmod(o * rows, tile_lanes)
        lane = lax.broadcasted_iota(jnp.int32, (cols, tile_lanes), 1)
        block = tri[:, base * tile_lanes:(base + 1) * tile_lanes]
        if off:
            block = pltpu.roll(block, tile_lanes - off, 1)
        if off + rows > tile_lanes:
            after = pltpu.roll(tri[:, (base + 1) * tile_lanes:(base + 2) * tile_lanes], tile_lanes - off, 1)
            block = jnp.where(lane < tile_lanes - off, block, after)
        top = jnp.where(lane[:ny] < rows, block[:ny], pltpu.roll(block[ny:two], rows, 1))
        return jnp.concatenate([top, block[two:]], 0)

    for g, (low, high) in enumerate(groups):
        if g == 0:
            take(b2l.at[0], rl.at[0])
            left_a = [nn_dot(swap1, b2l[x].reshape(nz * two, lanes)).astype(BF16) for x in range(2)]
            left_a = jnp.concatenate(left_a, 0)
        take_right(rx, 0, g, rr)
        panel_a, panel_b = panel(g)
        total = tn_dot(panel_a(), left_a)
        if g == 0:
            take(b2lf.at[0], rl.at[1])
            lefts = [jnp.concatenate([unfold(b2lf[x, k].astype(F32)) for k in range(nz)], 0) for x in range(2)]
            left_b = jnp.concatenate([nn_dot(swap2, left.astype(BF16)).astype(BF16) for left in lefts], 0)
        take_right(rxf, 1, g, rr)
        total = total + tn_dot(panel_b(), left_b)
        pp[low * rows:high * rows] = total[low * rows:high * rows]
        for k in range(low, high):
            send(pp.at[pl.ds(k * rows + (1 - core) * cols, cols)], qq.at[k], sq.at[g], rq.at[g], other_core)
        take(qq.at[pl.ds(low, high - low)], rq.at[g])
        for k in range(low, high):
            tri = (pp[pl.ds(k * rows + core * cols, cols), :] + qq[k]) * scale
            for o in range(ny):
                sc[k, o] = tile(tri, o).astype(BF16)
            for d in far_first(ny)[::-1]:
                to = at_y(d)
                send(sc.at[k, to], land.at[mine], s3, r3, (to * 2 + xh, k * 4 + xl * 2 + core))

            @pl.when(z != k)
            def _():
                send(sc.at[k, y], land.at[mine], s3, r3, dev_z(k))
    land[mine] = sc[z, y]

    for t in range(nt):
        gate[t] = jax.nn.sigmoid(nn_dot(normed[t], w_gate[...]))

    for part, (first, second, third) in enumerate(((a1l, a2l, rx), (a1lf, a2lf, rxf))):
        take(first.at[pl.ds(0, ny - 1)], s1l.at[part])
        take(first.at[pl.ds(0, nz - 1)], s1r.at[part])
        take(second.at[pl.ds(0, nz - 1)], s2l.at[part])
        take(second.at[pl.ds(0, ny - 1)], s2r.at[part])
        take(third.at[0], sl.at[part])

        for g in range(2):
            take_right(third, part, g, sr)
    for g, (low, high) in enumerate(groups):
        take(qq.at[pl.ds(low, high - low)], sq.at[g])

    take(land.at[pl.ds(0, chans - 1)], r3)
    f32[...] = land[...].astype(F32).reshape(f32.shape)
    picked = [f32[pl.ds(r, chans, stride=two), :] for r in range(two)]
    side = lax.broadcasted_iota(jnp.int32, picked[0].shape, 1) < rows
    for r in range(ny, two, 2):
        picked[r] = jnp.where(side, picked[r], pltpu.roll(picked[r + 1], rows, 1))
    places = [(r, r + ny) for r in range(ny)] + [(r, r + 1) for r in range(two, cols, 2)]
    mixed = tn_dot(jnp.concatenate(picked[:ny] + picked[ny::2], 1).astype(BF16), w_out[...])
    for index, pair_of in enumerate(places):
        for half, j in enumerate(pair_of):
            start = index * tile_lanes + half * rows
            t, at = j // ny, j % ny * rows
            out[j] = (gate[t, at:at + rows, :] * mixed[start:start + rows]).astype(BF16)

    take(land.at[pl.ds(0, chans - 1)], s3)


def per_device(ny, nz, pair, token_mask, ln_gain, ln_bias, w_left, w_right, w_gate, w_out):
    rows, cols, width = pair.shape
    lanes = ny * rows
    nt = cols // ny
    chans = ny * nz
    third = 2 * lanes // 3
    dma = pltpu.SemaphoreType.DMA
    swapped = pl.pallas_call(
        functools.partial(kernel, ny, nz),
        out_shape=pltpu.VMEM((cols, rows, width), BF16),
        in_specs=[pl.BlockSpec(memory_space=pl.ANY)] * 8,
        out_specs=pl.BlockSpec(memory_space=pltpu.VMEM),
        scratch_shapes=[
            pltpu.SMEM(token_mask.shape, jnp.int32),
            pltpu.VMEM((rows * cols, width), BF16),
            pltpu.VMEM((1, width), F32),
            pltpu.VMEM((1, width), F32),
            pltpu.VMEM(w_left.shape, BF16),
            pltpu.VMEM(w_right.shape, BF16),
            pltpu.VMEM(w_gate.shape, BF16),
            pltpu.VMEM(w_out.shape, BF16),
            dma((8,)),
            pltpu.VMEM((nt, rows * ny, width), F32),
            pltpu.VMEM((nt, rows * ny, width), BF16),
            pltpu.VMEM((nt, rows * ny, width), F32),
            pltpu.VMEM((4 * chans, width), BF16),
            pltpu.VMEM((ny, 2 * nz, lanes), BF16),
            pltpu.VMEM((ny, 2 * nz, third), BF16),
            pltpu.VMEM((ny, 2 * nz, lanes), BF16),
            pltpu.VMEM((ny, 2 * nz, third), BF16),
            pltpu.VMEM((nz, 2 * ny, lanes), BF16),
            pltpu.VMEM((nz, 2 * ny, third), BF16),
            pltpu.VMEM((nz, 2 * ny, lanes), BF16),
            pltpu.VMEM((nz, 2 * ny, third), BF16),
            pltpu.VMEM((nz, 2 * ny, lanes), BF16),
            pltpu.VMEM((nz, 2 * ny, third), BF16),
            pltpu.VMEM((2, nz, 2 * ny, lanes), BF16),
            pltpu.VMEM((2, nz, 2 * ny, third), BF16),
            pltpu.VMEM((ny, 2 * nz, lanes), BF16),
            pltpu.VMEM((ny, 2 * nz, third), BF16),
            pltpu.VMEM((ny, 2 * nz, lanes), BF16),
            pltpu.VMEM((ny, 2 * nz, third), BF16),
            pltpu.VMEM((2, ny, 2 * nz, lanes), BF16),
            pltpu.VMEM((2, ny, 2 * nz, third), BF16),
            pltpu.VMEM((lanes, lanes), F32),
            pltpu.VMEM((nz, cols, lanes), F32),
            pltpu.VMEM((nz, ny, 2 * ny, min(lanes, 128)), BF16),
            pltpu.VMEM((chans, 2 * ny, min(lanes, 128)), BF16),
            pltpu.VMEM((chans * 2 * ny, min(lanes, 128)), F32),
        ] + [dma((2,))] * 4 + [dma((2,)), dma((2, nz)), dma((2,)), dma((2, ny))] + [dma((2,))] * 2 + [dma((2, 2))] * 2 + [dma((2,))] * 2 + [dma] * 2,
        compiler_params=pltpu.CompilerParams(
            collective_id=0, has_side_effects=True, vmem_limit_bytes=60 * 1024 * 1024
        ),
    )(token_mask, pair.reshape(rows * cols, width), ln_gain.reshape(1, width), ln_bias.reshape(1, width), w_left, w_right, w_gate, w_out)
    return jnp.transpose(swapped, (1, 0, 2))


def solution(mesh):
    ny, nz = mesh.shape["row"] // 2, mesh.shape["col"] // 4
    placed = (P("row", "col", None), P(), P(), P(), P(), P(), P(), P())
    return jax.shard_map(
        functools.partial(per_device, ny, nz), mesh=mesh, in_specs=placed,
        out_specs=P("row", "col", None), check_vma=False,
    )
```

```python
import functools
import math

import jax
import jax.numpy as jnp
from jax import lax
from jax.experimental import pallas as pl
from jax.experimental.pallas import tpu as pltpu
from jax.sharding import PartitionSpec as P

F32 = jnp.float32
BF16 = jnp.bfloat16
MESH = pl.DeviceIdType.MESH


def one_hot(shape, source):
    row = lax.broadcasted_iota(jnp.int32, shape, 0)
    col = lax.broadcasted_iota(jnp.int32, shape, 1)
    return row, col, source(row)


def permutation(count, source):
    _, col, src = one_hot((count, count), source)
    return jnp.where(col == src, 1.0, 0.0).astype(BF16)


def swap_ends(a, b, c):
    return permutation(a * b * c, lambda o: (o % a) * (b * c) + ((o // a) % b) * c + o // (a * b))


def far_first(n):
    return sorted(range(1, n), key=lambda d: -min(d, n - d))


def nt_dot(x, y):
    return lax.dot_general(x, y, (((1,), (1,)), ((), ())), preferred_element_type=F32)


def tn_dot(x, y):
    return lax.dot_general(x, y, (((0,), (0,)), ((), ())), preferred_element_type=F32)


def nn_dot(x, y):
    return lax.dot_general(x, y, (((1,), (0,)), ((), ())), preferred_element_type=F32)


def spread(parts, width):
    return [pltpu.roll(part, y * width, 1) if y else part for y, part in enumerate(parts)]


def pick(rolled, width, k, keep=None):
    total = rolled[0].shape[1]
    n = total // width
    pos = lax.broadcasted_iota(jnp.int32, rolled[0].shape, 1) // width
    picked = rolled[0]
    for y, part in list(enumerate(rolled))[1:]:
        picked = jnp.where(pos == (k + y) % n, part, picked)
    return (pltpu.roll(picked, total - k * width, 1) if k else picked)[:, :keep]


def exchange(parts, width, keep=None):
    rolled = spread(parts, width)
    return [pick(rolled, width, k, keep) for k in range(parts[0].shape[1] // width)]


def fold(block):
    third = block.shape[1] // 3
    a, b, c = (block[:, i * third:(i + 1) * third] for i in range(3))
    return jnp.concatenate(
        [jnp.concatenate([a, b], 0), jnp.concatenate([c, jnp.zeros_like(c)], 0)], 1
    )


def unfold(block):
    n, third = block.shape[0] // 2, block.shape[1] // 2
    return jnp.concatenate([block[:n, :third], block[n:, :third], block[:n, third:]], 1)


def kernel(
    ny, nz, tm_hbm, pair_hbm, gain_hbm, bias_hbm, wl_hbm, wr_hbm, wg_hbm, wo_hbm, out,
    tm, pair, gain, bias, w_left, w_right, w_gate, w_out, load, n32, normed, gate, wt,
    a1l, a1lf, b1l, b1lf, a1r, a1rf, b1r, b1rf, a2l, a2lf, b2l, b2lf, a2r, a2rf, b2r, b2rf, rx, rxf,
    pp, qq, sc, land, f32,
    s1l, r1l, s1r, r1r, s2l, r2l, s2r, r2r, sl, rl, sr, rr, sq, rq, s3, r3,
):
    cols, rows, width = out.shape
    nt = cols // ny
    lanes = ny * rows
    chans = ny * nz
    loads = [
        pltpu.make_async_copy(src, dst, load.at[i])
        for i, (src, dst) in enumerate((
            (pair_hbm, pair), (wl_hbm, w_left), (wr_hbm, w_right), (tm_hbm, tm),
            (gain_hbm, gain), (bias_hbm, bias), (wg_hbm, w_gate), (wo_hbm, w_out),
        ))
    ]
    row, col = lax.axis_index("row"), lax.axis_index("col")
    y, xh = row // 2, row % 2
    z, xl, core = col // 4, (col // 2) % 2, col % 2
    same = xl == xh

    def at_y(d):
        return lax.rem(y + d, ny)

    def at_z(d):
        return lax.rem(z + d, nz)

    def dev_y(other):
        return (other * 2 + xh, col)

    def dev_z(other):
        return (row, other * 4 + xl * 2 + core)

    def dev_x(oh, ol):
        return (y * 2 + oh, z * 4 + ol * 2 + core)

    other_core = (row, z * 4 + xl * 2 + 1 - core)
    peers = [dev_y(at_y(d)) for d in far_first(ny)] + [dev_z(at_z(d)) for d in far_first(nz)]
    peers += [dev_x(xh, 1 - xl), dev_x(1 - xh, xl), dev_x(1 - xh, 1 - xl), other_core]
    barrier = pltpu.get_barrier_semaphore()
    for peer in peers:
        pl.semaphore_signal(barrier, inc=1, device_id=peer, device_id_type=MESH)

    for copy in loads:
        copy.start()

    def send(src, dst, send_sem, recv_sem, device):
        pltpu.make_async_remote_copy(
            src_ref=src, dst_ref=dst, send_sem=send_sem, recv_sem=recv_sem,
            device_id=device, device_id_type=MESH,
        ).start()

    def take(ref, sem):
        pltpu.make_async_copy(ref, ref, sem).wait()

    for copy in loads[1:]:
        copy.wait()

    _, c, r = one_hot((2 * chans, 2 * chans), lambda o: o)
    wt[0:2 * chans, :] = nt_dot(jnp.where(c == r, 1.0, 0.0).astype(BF16), w_left[...]).astype(BF16)
    _, c, r = one_hot(
        (2 * chans, 2 * chans), lambda o: (o // chans) * chans + (o % ny) * nz + (o % chans) // ny
    )
    wt[2 * chans:4 * chans, :] = nt_dot(jnp.where(c == r, 1.0, 0.0).astype(BF16), w_right[...]).astype(BF16)

    lane = lax.broadcasted_iota(jnp.int32, (1, lanes), 1)
    row_mask = jnp.zeros((1, lanes), F32)
    for i in range(rows):
        row_mask = jnp.where(lane % rows == i, tm[row * rows + i].astype(F32), row_mask)

    def mask_of(t):
        col_mask = jnp.zeros((1, lanes), F32)
        for k in range(ny):
            col_mask = jnp.where(lane // rows == k, tm[col * cols + t * ny + k].astype(F32), col_mask)
        return row_mask * col_mask

    def project(t):
        block = pair[...].astype(F32).reshape(rows, cols, width)[:, t * ny:(t + 1) * ny, :]
        center = jnp.mean(block, axis=-1, keepdims=True)
        delta = block - center
        spread = jnp.mean(delta * delta, axis=-1, keepdims=True)
        value = delta * lax.rsqrt(spread + 1e-05) * gain[...].reshape(1, 1, width) + bias[...].reshape(1, 1, width)
        n32[t] = value.reshape(rows * ny, width)
        for k in range(ny):
            normed[t, k * rows:(k + 1) * rows, :] = n32[t, pl.ds(k, rows, stride=ny), :].astype(BF16)
        proj = nt_dot(wt[...], normed[t])
        mask = mask_of(t)
        sides = (proj[:2 * chans], proj[2 * chans:])
        return [jax.nn.sigmoid(side[:chans]) * side[chans:] * mask for side in sides]

    swap1 = swap_ends(ny, 2, nz)
    swap2 = swap_ends(ny, 1, nz)

    def send_first(left, left_land, right, right_land, part):
        for d in far_first(ny):
            to = at_y(d)
            send(left.at[to], left_land.at[y], s1l.at[part], r1l.at[part], dev_y(to))
            to = at_z(d)
            send(right.at[to], right_land.at[z], s1r.at[part], r1r.at[part], dev_z(to))
        left_land[y] = left[y]
        right_land[z] = right[z]

    loads[0].wait()
    left0, right0 = project(0)
    left1, right1 = project(1)
    pairs = lambda u, v, n: jnp.concatenate([u.reshape(n, -1, lanes), v.reshape(n, -1, lanes)], 1).astype(BF16)
    a1l[...] = pairs(left0, left1, ny)
    a1r[...] = pairs(right0, right1, nz)
    left2, right2 = project(2)
    for k in range(ny):
        a1lf[k] = fold(left2[k * nz:(k + 1) * nz]).astype(BF16)
    for k in range(nz):
        a1rf[k] = fold(right2[k * ny:(k + 1) * ny]).astype(BF16)
    pl.semaphore_wait(barrier, len(peers))
    send_first(a1l, b1l, a1r, b1r, 0)
    send_first(a1lf, b1lf, a1rf, b1rf, 1)

    def turn_right(land, part, out_buf, dst):
        take(land.at[pl.ds(0, nz - 1)], r1r.at[part])
        out_buf[...] = nn_dot(swap1, land[...].reshape(nz * 2 * ny, -1)).astype(BF16).reshape(out_buf.shape)
        for d in far_first(ny):
            to = at_y(d)
            send(out_buf.at[to], dst.at[y], s2r.at[part], r2r.at[part, y], dev_y(to))
        dst[y] = out_buf[y]

    def send_left(out_buf, dst, part):
        for d in far_first(nz):
            to = at_z(d)
            send(out_buf.at[to], dst.at[xl, z], s2l.at[part], r2l.at[part, z], dev_z(to))
        dst[xl, z] = out_buf[z]

    take(b1l.at[pl.ds(0, ny - 1)], r1l.at[0])
    parts = exchange([b1l[k].astype(F32) for k in range(ny)], rows)
    a2l[...] = nn_dot(swap1, jnp.concatenate(parts, 0).astype(BF16)).astype(BF16).reshape(a2l.shape)
    send_left(a2l, b2l, 0)
    turn_right(b1r, 0, a2r, b2r)
    take(b1lf.at[pl.ds(0, ny - 1)], r1l.at[1])
    parts = exchange([unfold(b1lf[k].astype(F32)) for k in range(ny)], rows)
    turned = nn_dot(swap2, jnp.concatenate(parts, 0).astype(BF16))
    for k in range(nz):
        a2lf[k] = fold(turned[k * ny:(k + 1) * ny]).astype(BF16)
    send_left(a2lf, b2lf, 1)
    def forward_left(left, part, k):
        send(left.at[xl, k], left.at[xl, k], sl.at[part], rl.at[part], dev_x(xh, 1 - xl))

    forward_left(b2l, 0, z)
    turn_right(b1rf, 1, a2rf, b2rf)

    ahead = max(1, lanes // (3 * rows))
    cut = -(-ahead * rows * 3 // lanes) * (lanes // 3)
    groups = ((0, ahead), (ahead, nz))

    def forward_right(right, dst, part, g):
        low, high = groups[g]
        for k in range(low, high):
            @pl.when(y != k)
            def _():
                take(right.at[k], r2r.at[part, k])

            send(right.at[k], dst.at[xl, k], sr.at[part, g], rr.at[part, g], dev_x(1 - xh, xh))

            @pl.when(jnp.logical_not(same))
            def _():
                send(right.at[k], dst.at[xl, k], sr.at[part, g], rr.at[part, g], dev_x(xh, xh))

        @pl.when(same)
        def _():
            dst[xl, low:high] = right[low:high]

    for part, (left, right, dst) in enumerate(((b2l, b2r, rx), (b2lf, b2rf, rxf))):
        if part:
            forward_left(left, part, z)
        order = far_first(nz)[::-1]
        for place, d in enumerate(order):
            if place == len(order) // 2:
                forward_right(right, dst, part, 0)
            k = at_z(d)
            take(left.at[xl, k], r2l.at[part, k])
            forward_left(left, part, k)
    forward_right(b2r, rx, 0, 1)
    forward_right(b2rf, rxf, 1, 1)

    two = 2 * ny

    def take_right(dst, part, g, sem):
        low, high = groups[g]

        @pl.when(same)
        def _():
            take(dst.at[0, pl.ds(low, high - low)], sem.at[part, g])

        @pl.when(jnp.logical_not(same))
        def _():
            take(dst.at[:, pl.ds(low, high - low)], sem.at[part, g])

    def panel(g):
        count, keep = (ahead, cut) if g == 0 else (ny, lanes)

        def stack(parts):
            return jnp.concatenate(exchange(parts, rows, keep), 0).astype(BF16)

        return (
            lambda: jnp.concatenate([stack([rx[x, k].astype(F32) for k in range(count)]) for x in range(2)], 0),
            lambda: jnp.concatenate(
                [stack([unfold(rxf[x, k].astype(F32)) for k in range(count)]) for x in range(2)], 0
            ),
        )

    scale = 4.0 / math.sqrt(rows * 2 * ny)
    mine = y * nz + z
    tile_lanes = land.shape[2]

    def tile(tri, o):
        base, off = divmod(o * rows, tile_lanes)
        lane = lax.broadcasted_iota(jnp.int32, (cols, tile_lanes), 1)
        block = tri[:, base * tile_lanes:(base + 1) * tile_lanes]
        if off:
            block = pltpu.roll(block, tile_lanes - off, 1)
        if off + rows > tile_lanes:
            after = pltpu.roll(tri[:, (base + 1) * tile_lanes:(base + 2) * tile_lanes], tile_lanes - off, 1)
            block = jnp.where(lane < tile_lanes - off, block, after)
        top = jnp.where(lane[:ny] < rows, block[:ny], pltpu.roll(block[ny:two], rows, 1))
        return jnp.concatenate([top, block[two:]], 0)

    for g, (low, high) in enumerate(groups):
        if g == 0:
            take(b2l.at[0], rl.at[0])
            left_a = [nn_dot(swap1, b2l[x].reshape(nz * two, lanes)).astype(BF16) for x in range(2)]
            left_a = jnp.concatenate(left_a, 0)
        take_right(rx, 0, g, rr)
        panel_a, panel_b = panel(g)
        total = tn_dot(panel_a(), left_a)
        if g == 0:
            take(b2lf.at[0], rl.at[1])
            lefts = [jnp.concatenate([unfold(b2lf[x, k].astype(F32)) for k in range(nz)], 0) for x in range(2)]
            left_b = jnp.concatenate([nn_dot(swap2, left.astype(BF16)).astype(BF16) for left in lefts], 0)
        take_right(rxf, 1, g, rr)
        total = total + tn_dot(panel_b(), left_b)
        pp[low * rows:high * rows] = total[low * rows:high * rows]
        for k in range(low, high):
            send(pp.at[pl.ds(k * rows + (1 - core) * cols, cols)], qq.at[k], sq.at[g], rq.at[g], other_core)
        take(qq.at[pl.ds(low, high - low)], rq.at[g])
        for k in range(low, high):
            tri = (pp[pl.ds(k * rows + core * cols, cols), :] + qq[k]) * scale
            for o in range(ny):
                sc[k, o] = tile(tri, o).astype(BF16)
            for d in far_first(ny)[::-1]:
                to = at_y(d)
                send(sc.at[k, to], land.at[mine], s3, r3, (to * 2 + xh, k * 4 + xl * 2 + core))

            @pl.when(z != k)
            def _():
                send(sc.at[k, y], land.at[mine], s3, r3, dev_z(k))
    land[mine] = sc[z, y]

    for t in range(nt):
        gate[t] = jax.nn.sigmoid(nn_dot(normed[t], w_gate[...]))

    for part, (first, second, third) in enumerate(((a1l, a2l, rx), (a1lf, a2lf, rxf))):
        take(first.at[pl.ds(0, ny - 1)], s1l.at[part])
        take(first.at[pl.ds(0, nz - 1)], s1r.at[part])
        take(second.at[pl.ds(0, nz - 1)], s2l.at[part])
        take(second.at[pl.ds(0, ny - 1)], s2r.at[part])
        take(third.at[0], sl.at[part])

        for g in range(2):
            take_right(third, part, g, sr)
    for g, (low, high) in enumerate(groups):
        take(qq.at[pl.ds(low, high - low)], sq.at[g])

    take(land.at[pl.ds(0, chans - 1)], r3)
    f32[...] = land[...].astype(F32).reshape(f32.shape)
    picked = [f32[pl.ds(r, chans, stride=two), :] for r in range(two)]
    side = lax.broadcasted_iota(jnp.int32, picked[0].shape, 1) < rows
    for r in range(ny, two, 2):
        picked[r] = jnp.where(side, picked[r], pltpu.roll(picked[r + 1], rows, 1))
    places = [(r, r + ny) for r in range(ny)] + [(r, r + 1) for r in range(two, cols, 2)]
    mixed = tn_dot(jnp.concatenate(picked[:ny] + picked[ny::2], 1).astype(BF16), w_out[...])
    for index, pair_of in enumerate(places):
        for half, j in enumerate(pair_of):
            start = index * tile_lanes + half * rows
            t, at = j // ny, j % ny * rows
            out[j] = (gate[t, at:at + rows, :] * mixed[start:start + rows]).astype(BF16)

    take(land.at[pl.ds(0, chans - 1)], s3)


def per_device(ny, nz, pair, token_mask, ln_gain, ln_bias, w_left, w_right, w_gate, w_out):
    rows, cols, width = pair.shape
    lanes = ny * rows
    nt = cols // ny
    chans = ny * nz
    third = 2 * lanes // 3
    dma = pltpu.SemaphoreType.DMA
    swapped = pl.pallas_call(
        functools.partial(kernel, ny, nz),
        out_shape=pltpu.VMEM((cols, rows, width), BF16),
        in_specs=[pl.BlockSpec(memory_space=pl.ANY)] * 8,
        out_specs=pl.BlockSpec(memory_space=pltpu.VMEM),
        scratch_shapes=[
            pltpu.SMEM(token_mask.shape, jnp.int32),
            pltpu.VMEM((rows * cols, width), BF16),
            pltpu.VMEM((1, width), F32),
            pltpu.VMEM((1, width), F32),
            pltpu.VMEM(w_left.shape, BF16),
            pltpu.VMEM(w_right.shape, BF16),
            pltpu.VMEM(w_gate.shape, BF16),
            pltpu.VMEM(w_out.shape, BF16),
            dma((8,)),
            pltpu.VMEM((nt, rows * ny, width), F32),
            pltpu.VMEM((nt, rows * ny, width), BF16),
            pltpu.VMEM((nt, rows * ny, width), F32),
            pltpu.VMEM((4 * chans, width), BF16),
            pltpu.VMEM((ny, 2 * nz, lanes), BF16),
            pltpu.VMEM((ny, 2 * nz, third), BF16),
            pltpu.VMEM((ny, 2 * nz, lanes), BF16),
            pltpu.VMEM((ny, 2 * nz, third), BF16),
            pltpu.VMEM((nz, 2 * ny, lanes), BF16),
            pltpu.VMEM((nz, 2 * ny, third), BF16),
            pltpu.VMEM((nz, 2 * ny, lanes), BF16),
            pltpu.VMEM((nz, 2 * ny, third), BF16),
            pltpu.VMEM((nz, 2 * ny, lanes), BF16),
            pltpu.VMEM((nz, 2 * ny, third), BF16),
            pltpu.VMEM((2, nz, 2 * ny, lanes), BF16),
            pltpu.VMEM((2, nz, 2 * ny, third), BF16),
            pltpu.VMEM((ny, 2 * nz, lanes), BF16),
            pltpu.VMEM((ny, 2 * nz, third), BF16),
            pltpu.VMEM((ny, 2 * nz, lanes), BF16),
            pltpu.VMEM((ny, 2 * nz, third), BF16),
            pltpu.VMEM((2, ny, 2 * nz, lanes), BF16),
            pltpu.VMEM((2, ny, 2 * nz, third), BF16),
            pltpu.VMEM((lanes, lanes), F32),
            pltpu.VMEM((nz, cols, lanes), F32),
            pltpu.VMEM((nz, ny, 2 * ny, min(lanes, 128)), BF16),
            pltpu.VMEM((chans, 2 * ny, min(lanes, 128)), BF16),
            pltpu.VMEM((chans * 2 * ny, min(lanes, 128)), F32),
        ] + [dma((2,))] * 4 + [dma((2,)), dma((2, nz)), dma((2,)), dma((2, ny))] + [dma((2,))] * 2 + [dma((2, 2))] * 2 + [dma((2,))] * 2 + [dma] * 2,
        compiler_params=pltpu.CompilerParams(
            collective_id=0, has_side_effects=True, vmem_limit_bytes=60 * 1024 * 1024
        ),
    )(token_mask, pair.reshape(rows * cols, width), ln_gain.reshape(1, width), ln_bias.reshape(1, width), w_left, w_right, w_gate, w_out)
    return jnp.transpose(swapped, (1, 0, 2))


def solution(mesh):
    ny, nz = mesh.shape["row"] // 2, mesh.shape["col"] // 4
    placed = (P("row", "col", None), P(), P(), P(), P(), P(), P(), P())
    return jax.shard_map(
        functools.partial(per_device, ny, nz), mesh=mesh, in_specs=placed,
        out_specs=P("row", "col", None), check_vma=False,
    )
```
